32 devices in a mesh: segment: 2 (over y), rows: 4 (over z), dp: 4 (over x, core).
Axes of the slice: x: 2, y: 2, z: 4, core: 2. Of those that a mesh axis runs over, the one named last changes fastest.
Arguments:
- clips: bfloat16 [4, 4, 4, 32, 8, 128], P(None, 'dp', None, 'rows'), may hold values from -80 to 80
- lengths: int32 [4, 4], P(None, 'dp'), may hold values from 1 to 4, as said below
- conv_weight: bfloat16 [2, 3456, 128], P('segment'), may hold values from -0.109375 to 0.109375
- norm_gain: float32 [2, 128], P('segment'), may hold values from 0.5 to 2
- norm_shift: float32 [2, 128], P('segment'), may hold values from -1 to 1
- conv_bias: float32 [2, 128], P('segment'), may hold values from -3 to 3
- cotangent: bfloat16 [2, 4, 4, 4, 32, 8, 128], P('segment', None, 'dp', None, 'rows'), may hold values from -6 to 6
Outputs:
- stash: bfloat16 [2, 4, 4, 4, 32, 8, 128], P('segment', None, 'dp', None, 'rows')
- weight_grad: float32 [2, 3456, 128], P('segment')
The draws below stay inside these ranges and needn't reach their ends.
Inputs may be any that keep to these rules, and one draw needn't show every extreme that they name: lengths[m, clip] real frames lead each clip; the frames after them are padding; some clip has all 4 frames.
All inputs are finite; a program needn't handle non-finite values.
Results may differ from the reference program's by a relative error of at most 0.009.
Values may be sent and summed in bfloat16 or wider, within the bound.
No kernel may reach another device: no remote copies, remote signals or barrier semaphores. Data moves between devices by JAX's collectives and lax.ppermute only.
A program may use at most 64 MiB of HBM per device.

```python
import math
import jax
import jax.numpy as jnp
from jax import lax

C = 128
GROUPS = 32
MB = 4
FRAMES = 4
COLS = 8
SEGMENTS = 2
CLIPS = 4
HEIGHT = 32


def draw_clips(key, part):
    keys = jax.random.split(key, 3)
    place = jnp.arange(HEIGHT, dtype=jnp.float32) / max(HEIGHT - 1, 1)
    shape = (MB, CLIPS, FRAMES, HEIGHT, COLS, C)
    rise = jnp.exp(jnp.log(3.0) * place)
    noise = jnp.clip(jax.random.normal(keys[0], shape, jnp.float32), -5.0, 5.0)
    chan = jnp.exp(jax.random.uniform(keys[1], (C,), jnp.float32, jnp.log(0.5), jnp.log(2.0)))
    offset = jnp.clip(0.5 * jax.random.normal(keys[2], (MB, CLIPS, 1, 1, 1, C), jnp.float32), -1.0, 1.0)
    return (rise[None, None, None, :, None, None] * (offset + chan * noise)).astype(jnp.bfloat16)


def draw_lengths(key, part):
    first, second = jax.random.split(key)
    counts = jax.random.randint(first, (MB * CLIPS,), 1, FRAMES + 1)
    full_at = jax.random.randint(second, (), 0, MB * CLIPS)
    counts = jnp.where(jnp.arange(MB * CLIPS) == full_at, FRAMES, counts)
    return counts.reshape(MB, CLIPS).astype(jnp.int32)


def block_levels(rng, shape, cuts, least, top_value):
    def one(dim, shards_of):
        steps = jax.random.uniform(jax.random.fold_in(jax.random.fold_in(rng, 6), dim), (shards_of,), jnp.float32, least / len(cuts), top_value / len(cuts))
        return jnp.repeat(jnp.exp(steps), shape[dim] // shards_of).reshape((-1,) + (1,) * (len(shape) - dim - 1))

    factor_of = one(*cuts[0])
    for cut in cuts[1:]:
        factor_of = factor_of * one(*cut)
    return factor_of


def centred(rng, extent, deviation, most, cuts=(), kind=jnp.bfloat16):
    factor_of = block_levels(rng, extent, cuts, -0.22, 0.18) if cuts else 1.0
    drawn = jax.random.normal(rng, extent, jnp.float32) * deviation * factor_of
    return jnp.minimum(jnp.maximum(drawn, -most), most).astype(kind)


def setup_inputs(seed: int = 0) -> dict:
    key_list = jax.random.split(jax.random.key(seed), 8)
    return {
        "clips": draw_clips(jax.random.fold_in(key_list[7], 71), 0),
        "lengths": draw_lengths(jax.random.fold_in(key_list[7], 71), 0),
        "conv_weight": centred(key_list[2], (SEGMENTS, 27 * C, C), (27 * C) ** -0.5, 0.109375, ((0, 2),)),
        "norm_gain": jnp.clip(jnp.exp(math.log(2.0) - 1.3862944 * jax.random.uniform(key_list[3], (SEGMENTS, C), jnp.float32) ** block_levels(key_list[3], (SEGMENTS, C), ((0, 2),), -0.2, 0.2)), 0.5, 2.0),
        "norm_shift": jnp.clip(jax.random.uniform(key_list[4], (SEGMENTS, C), jnp.float32, -1.0, 1.0) * block_levels(key_list[4], (SEGMENTS, C), ((0, 2),), -0.4, 0.0), -1.0, 1.0),
        "conv_bias": centred(key_list[5], (SEGMENTS, C), 0.5, 3.0, ((0, 2),), jnp.float32),
        "cotangent": centred(key_list[6], (SEGMENTS, MB, CLIPS, FRAMES, HEIGHT, COLS, C), 1.0, 6.0, ((0, 2), (2, 4), (4, 4))),
    }


eps = 1e-06

def block(inputs, length, weight, gain, shift, bias):
    clip_count, frames, height, cols, chans = inputs.shape
    sub = chans // GROUPS
    values = inputs.astype(jnp.float32)
    mask = (jnp.arange(frames)[None, :] < length[:, None]).astype(jnp.float32)
    mask_six = mask[:, :, None, None, None, None]
    grouped = values.reshape(clip_count, frames, height, cols, GROUPS, sub)
    count = (length * (height * cols * sub)).astype(jnp.float32)[:, None]
    mean = lax.optimization_barrier(jnp.sum(grouped * mask_six, axis=(1, 2, 3, 5))) / count
    centered = grouped - mean[:, None, None, None, :, None]
    var = lax.optimization_barrier(jnp.sum(centered * centered * mask_six, axis=(1, 2, 3, 5))) / count
    rstd = lax.rsqrt(var + eps)
    normed = (centered * rstd[:, None, None, None, :, None]).reshape(values.shape) * gain + shift
    hidden = jax.nn.silu(normed).astype(jnp.bfloat16)
    padded = jnp.pad(hidden, ((0, 0), (0, 0), (1, 1), (1, 1), (0, 0)))
    padded = jnp.concatenate([padded[:, :1], padded[:, :1], padded], axis=1)
    pieces = []
    for tap_t in range(3):
        for tap_h in range(3):
            for tap_w in range(3):
                pieces.append(padded[:, tap_t:tap_t + frames, tap_h:tap_h + height, tap_w:tap_w + cols, :])
    patches = jnp.concatenate(pieces, axis=-1).reshape(-1, 27 * chans)
    conv = jnp.dot(patches, weight, preferred_element_type=jnp.float32).reshape(values.shape)
    mask_five = mask[:, :, None, None, None]
    result = ((values + conv + bias) * mask_five).astype(jnp.bfloat16)
    return (result, patches, mask_five.astype(jnp.bfloat16))

def reference(clips, lengths, conv_weight, norm_gain, norm_shift, conv_bias, cotangent):
    scale = 1.0 / math.sqrt(MB * CLIPS * FRAMES * HEIGHT * COLS)

    def one_batch(grads, inputs):
        current, length, cot = inputs
        outputs = []
        updated = []
        for segment in range(SEGMENTS):
            current, patches, mask_five = block(current, length, conv_weight[segment], norm_gain[segment], norm_shift[segment], conv_bias[segment])
            outputs.append(current)
            masked = (cot[segment] * mask_five).reshape(-1, C)
            term = lax.dot_general(patches, masked, (((0,), (0,)), ((), ())), preferred_element_type=jnp.float32)
            updated.append(grads[segment] + term)
        return (jnp.stack(updated), jnp.stack(outputs))
    start = jnp.zeros((SEGMENTS, 27 * C, C), jnp.float32)
    grads, stash = lax.scan(one_batch, start, (clips, lengths, jnp.moveaxis(cotangent, 1, 0)))
    return (jnp.moveaxis(stash, 0, 1), grads * scale)
```

```python
import math

import jax
import jax.numpy as jnp
from jax import lax
from jax.sharding import PartitionSpec as P

GROUPS = 32


eps = 1e-06


def extended_2(cells, sides, width):
    for axis, dim in sides:
        count = lax.axis_size(axis)
        ends = count - 1
        head = lax.slice_in_dim(cells, 0, width, axis=dim)
        tail = lax.slice_in_dim(cells, cells.shape[dim] - width, cells.shape[dim], axis=dim)
        cells = jnp.concatenate(
            [
                lax.ppermute(tail, axis, [(i, (i + 1) % count) for i in range(ends)]),
                cells,
                lax.ppermute(head, axis, [((i + 1) % count, i) for i in range(ends)]),
            ],
            axis=dim,
        )
    return cells


def passed_along(block, axis, distance):
    devices = range(lax.axis_size(axis))
    route = [(i - distance, i) for i in devices if i - distance in devices]
    return lax.ppermute(block, axis, route)


def statistics(values, frame_mask, length, height):
    clip_count, frames, rows_here, cols, chans = values.shape
    sub = chans // GROUPS
    grouped = values.reshape(clip_count, frames, rows_here, cols, GROUPS, sub)
    mask_six = frame_mask[:, :, :, :, :, None]
    count = (length * (height * cols * sub)).astype(jnp.float32)[:, None]
    total = lax.psum(jnp.sum(grouped * mask_six, axis=(1, 2, 3, 5)), "rows")
    mean = total / count
    centered = grouped - mean[:, None, None, None, :, None]
    spread = lax.psum(jnp.sum(centered * centered * mask_six, axis=(1, 2, 3, 5)), "rows")
    var = spread / count
    rstd = lax.rsqrt(var + eps)
    mean_chan = jnp.repeat(mean, sub, axis=-1)[:, None, None, None, :]
    rstd_chan = jnp.repeat(rstd, sub, axis=-1)[:, None, None, None, :]
    return (mean_chan, rstd_chan)


def block(current, length, weight, gain, shift, bias, height):
    clip_count, frames, rows_here, cols, chans = current.shape
    values = current.astype(jnp.float32)
    frame_mask = (jnp.arange(frames)[None, :] < length[:, None]).astype(jnp.float32)[
        :, :, None, None, None
    ]
    mean_chan, rstd_chan = statistics(values, frame_mask, length, height)
    hidden = jax.nn.silu((values - mean_chan) * rstd_chan * gain + shift).astype(jnp.bfloat16)
    extended = extended_2(hidden, (("rows", 2),), 1)
    padded = jnp.pad(extended, ((0, 0), (0, 0), (0, 0), (1, 1), (0, 0)))
    padded = jnp.concatenate([padded[:, :1], padded[:, :1], padded], axis=1)
    pieces = []
    for tap_t in range(3):
        for tap_h in range(3):
            for tap_w in range(3):
                pieces.append(
                    padded[
                        :,
                        tap_t : tap_t + frames,
                        tap_h : tap_h + rows_here,
                        tap_w : tap_w + cols,
                        :,
                    ]
                )
    patches = jnp.concatenate(pieces, axis=-1).reshape(-1, 27 * chans)
    conv = jnp.dot(patches, weight, preferred_element_type=jnp.float32).reshape(values.shape)
    result = ((values + conv + bias) * frame_mask).astype(jnp.bfloat16)
    return (result, patches, frame_mask.astype(jnp.bfloat16))


def relay(clips, lengths, conv_weight, norm_gain, norm_shift, conv_bias, cotangent):
    segments = lax.axis_size("segment")
    segment_id = lax.axis_index("segment")
    micro = clips.shape[0]
    frames = clips.shape[2]
    cols = clips.shape[4]
    chans = clips.shape[5]
    height = clips.shape[3] * lax.axis_size("rows")
    weight = conv_weight[0]
    gain = norm_gain[0]
    shift = norm_shift[0]
    bias = conv_bias[0]
    cot_all = cotangent[0]
    total_cells = micro * clips.shape[1] * lax.axis_size("dp") * frames * height * cols
    factor = 1.0 / math.sqrt(total_cells)

    def tick(step, carry):
        arrived, stash, grads = carry
        which = step - segment_id
        valid = (which >= 0) & (which < micro)
        slot = jnp.clip(which, 0, micro - 1)
        fresh = lax.dynamic_index_in_dim(
            clips, jnp.clip(step, 0, micro - 1).astype(jnp.int32), 0, keepdims=False
        )
        current = jnp.where(segment_id == 0, fresh, arrived)
        length = lax.dynamic_index_in_dim(lengths, slot, 0, keepdims=False)
        result, patches, mask_five = block(current, length, weight, gain, shift, bias, height)
        cot_now = lax.dynamic_index_in_dim(cot_all, slot, 0, keepdims=False)
        masked = (cot_now * mask_five).reshape(-1, chans)
        term = lax.dot_general(
            patches, masked, (((0,), (0,)), ((), ())), preferred_element_type=jnp.float32
        )
        grads = grads + jnp.where(valid, term, 0.0)
        previous = lax.dynamic_index_in_dim(stash, slot, 0, keepdims=False)
        stash = lax.dynamic_update_index_in_dim(stash, jnp.where(valid, result, previous), slot, 0)
        arrived = passed_along(result, "segment", 1)
        return (arrived, stash, grads)

    start = (
        jnp.zeros(clips.shape[1:], jnp.bfloat16),
        jnp.zeros(clips.shape, jnp.bfloat16),
        jnp.zeros((27 * chans, chans), jnp.float32),
    )
    arrived, stash, grads = lax.fori_loop(0, micro + segments - 1, tick, start)
    grads = lax.psum(grads, ("rows", "dp")) * factor
    return (stash[None], grads[None])


def swapped(value, axis, flip):
    return lax.ppermute(value, axis, [(i, i ^ flip) for i in range(lax.axis_size(axis))])


def two(own, other, bit):
    return jnp.where(bit == 0, jnp.stack([own, other]), jnp.stack([other, own]))


def by_index(pieces, me):
    count = len(pieces)
    stacked = jnp.stack(pieces)
    return jnp.stack(
        [lax.dynamic_index_in_dim(stacked, me ^ i, 0, keepdims=False) for i in range(count)]
    )


def split_three(value):
    high = lax.reduce_precision(value, 8, 7)
    rest = value - high
    middle = lax.reduce_precision(rest, 8, 7)
    return jnp.stack([high, middle, rest - middle]).astype(jnp.bfloat16)


def normalized(values, length, gain, shift):
    frames, height, cols, chans = values.shape
    sub = chans // GROUPS
    values = values.astype(jnp.float32)
    mask = (jnp.arange(frames) < length).astype(jnp.float32)[:, None, None, None, None]
    grouped = values.reshape(frames, height, cols, GROUPS, sub)
    count = (length * (height * cols * sub)).astype(jnp.float32)
    mean = jnp.sum(grouped * mask, axis=(0, 1, 2, 4)) / count
    centered = grouped - mean[:, None]
    var = jnp.sum(centered * centered * mask, axis=(0, 1, 2, 4)) / count
    normed = (centered * lax.rsqrt(var + eps)[:, None]).reshape(values.shape) * gain + shift
    return jax.nn.silu(normed).astype(jnp.bfloat16)


def patches_of(hidden):
    frames, height, cols, chans = hidden.shape[-4:]
    lead = [(0, 0)] * (hidden.ndim - 4)
    padded = jnp.pad(hidden, lead + [(2, 0), (1, 1), (1, 1), (0, 0)])
    first = hidden[..., :1, :, :, :]
    padded = jnp.pad(hidden, lead + [(0, 0), (1, 1), (1, 1), (0, 0)])
    padded = jnp.concatenate([padded[..., :1, :, :, :], padded[..., :1, :, :, :], padded], axis=-4)
    pieces = [
        padded[..., a : a + frames, b : b + height, d : d + cols, :]
        for a in range(3)
        for b in range(3)
        for d in range(3)
    ]
    return jnp.concatenate(pieces, axis=-1).reshape(-1, 27 * chans)


def whole_clips(clips, lengths, conv_weight, norm_gain, norm_shift, conv_bias, cotangent):
    segment = lax.axis_index("segment")
    row = lax.axis_index("rows")
    part = lax.axis_index("dp")
    micro, _, frames, rows_here, cols, chans = clips.shape
    height = rows_here * micro
    total_cells = micro * lax.axis_size("dp") * frames * height * cols
    factor = 1.0 / math.sqrt(total_cells)
    core = part & 1
    weight = conv_weight[0]
    half = weight.shape[0] // 2

    extras = split_three(jnp.concatenate([norm_gain, norm_shift, conv_bias])).reshape(9, chans)
    extras = jnp.pad(extras, ((0, 7), (0, 0)))
    mine = lax.dynamic_slice_in_dim(weight, core * half, half)
    arrived = lax.ppermute(jnp.concatenate([mine, extras]), "segment", [(0, 1)])

    def to_clips(value):
        pieces = [
            lax.dynamic_index_in_dim(value, row ^ k, 0, keepdims=False) for k in range(micro)
        ]
        pieces = [pieces[0]] + [swapped(pieces[k], "rows", k) for k in range(1, micro)]
        whole = jnp.moveaxis(by_index(pieces, row), 0, 1)
        return whole.reshape(frames, height, cols, chans)

    current = to_clips(clips[:, 0])
    length = lax.dynamic_index_in_dim(lengths[:, 0], row, 0, keepdims=False)
    mask = (jnp.arange(frames) < length).astype(jnp.float32)[:, None, None, None]
    cot = to_clips(cotangent[0, :, 0]) * mask.astype(jnp.bfloat16)
    cot = two(cot, swapped(cot, "dp", 2), part >> 1)
    cot = jnp.swapaxes(two(cot, swapped(cot, "dp", 1), core), 0, 1)
    cot = cot.reshape(-1, chans)

    other = swapped(arrived, "dp", 1)
    first_weight = two(arrived[:half], other[:half], core).reshape(weight.shape)
    first_weight = jnp.where(segment == 0, weight, first_weight)
    first = jnp.sum(arrived[half : half + 9].astype(jnp.float32).reshape(3, 3, chans), axis=0)
    gain0 = jnp.where(segment == 0, norm_gain[0], first[0])
    shift0 = jnp.where(segment == 0, norm_shift[0], first[1])
    bias0 = jnp.where(segment == 0, conv_bias[0], first[2])

    def conv(value, hidden, weight, bias):
        out = jnp.dot(patches_of(hidden), weight, preferred_element_type=jnp.float32)
        out = value.astype(jnp.float32) + out.reshape(value.shape) + bias
        return (out * mask).astype(jnp.bfloat16)

    hidden0 = normalized(current, length, gain0, shift0)
    middle = conv(current, hidden0, first_weight, bias0)
    hidden1 = normalized(middle, length, norm_gain[0], norm_shift[0])
    hidden = jnp.where(segment == 0, hidden0, hidden1)

    quarter = chans // 4
    slices = jnp.moveaxis(hidden.reshape(frames, height, cols, 4, quarter), 3, 0)
    slices = slices.reshape(4, frames, height * cols, quarter)
    slices = jnp.moveaxis(slices, 1, 2).reshape(4, height * cols, frames * quarter)
    pieces = [lax.dynamic_index_in_dim(slices, part ^ k, 0, keepdims=False) for k in range(4)]
    pieces = [pieces[0]] + [swapped(pieces[k], "dp", k) for k in range(1, 4)]
    held = by_index(pieces, part).reshape(4, height, cols, frames, quarter)
    held = jnp.moveaxis(held, 3, 1)

    last = conv(middle, hidden1, weight, conv_bias[0])
    stash = jnp.where(segment == 0, middle, last)

    grad = lax.dot_general(
        patches_of(held), cot, (((0,), (0,)), ((), ())), preferred_element_type=jnp.float32
    )
    grad = grad.astype(jnp.bfloat16).reshape(27, 2, 2, quarter // 4, chans)
    grad = jnp.moveaxis(grad, 0, 2).reshape(2, 2, 27 * quarter // 4, chans)
    low, high = row & 1, row >> 1
    keep = jnp.where(low == 0, grad[:, 0], grad[:, 1])
    send = jnp.where(low == 0, grad[:, 1], grad[:, 0])
    total = keep.astype(jnp.float32) + swapped(send, "rows", 1).astype(jnp.float32)
    keep = jnp.where(high == 0, total[0], total[1])
    send = jnp.where(high == 0, total[1], total[0]).astype(jnp.bfloat16)
    total = keep + swapped(send, "rows", 2).astype(jnp.float32)
    total = (total * factor).astype(jnp.bfloat16)
    total = two(total, swapped(total, "rows", 2), high)
    total = jnp.swapaxes(two(total, swapped(total, "rows", 1), low), 0, 1)
    total = two(total, swapped(total, "dp", 2), part >> 1)
    total = jnp.swapaxes(two(total, swapped(total, "dp", 1), core), 0, 1)
    total = total.reshape(4, 4, 27, quarter // 4, chans)
    grads = jnp.transpose(total, (2, 0, 1, 3, 4)).reshape(27 * chans, chans).astype(jnp.float32)

    back = jnp.moveaxis(stash.reshape(frames, micro, rows_here, cols, chans), 1, 0)
    pieces = [lax.dynamic_index_in_dim(back, row ^ k, 0, keepdims=False) for k in range(micro)]
    pieces = [pieces[0]] + [swapped(pieces[k], "rows", k) for k in range(1, micro)]
    stash = by_index(pieces, row)[:, None]
    return (stash[None], grads[None])


def per_device(clips, lengths, conv_weight, norm_gain, norm_shift, conv_bias, cotangent):
    sizes = [lax.axis_size(axis) for axis in ("segment", "rows", "dp")]
    fits = sizes == [2, 4, 4] and clips.shape[0] == 4 and clips.shape[1] == 1
    plan = whole_clips if fits and clips.shape[5] == 128 else relay
    return plan(clips, lengths, conv_weight, norm_gain, norm_shift, conv_bias, cotangent)


def solution(mesh):
    in_specs = (
        P(None, "dp", None, "rows", None, None),
        P(None, "dp"),
        P("segment", None, None),
        P("segment", None),
        P("segment", None),
        P("segment", None),
        P("segment", None, "dp", None, "rows", None, None),
    )
    out_specs = (P("segment", None, "dp", None, "rows", None, None), P("segment", None, None))
    return jax.shard_map(
        per_device, mesh=mesh, in_specs=in_specs, out_specs=out_specs, check_vma=False
    )
```

```python
import functools
import math

import jax
import jax.numpy as jnp
from jax import lax
from jax.experimental import pallas as pl
from jax.experimental.pallas import tpu as pltpu
from jax.sharding import PartitionSpec as P

GROUPS = 32


eps = 1e-06


def extended_2(cells, sides, width):
    for axis, dim in sides:
        count = lax.axis_size(axis)
        ends = count - 1
        head = lax.slice_in_dim(cells, 0, width, axis=dim)
        tail = lax.slice_in_dim(cells, cells.shape[dim] - width, cells.shape[dim], axis=dim)
        cells = jnp.concatenate(
            [
                lax.ppermute(tail, axis, [(i, (i + 1) % count) for i in range(ends)]),
                cells,
                lax.ppermute(head, axis, [((i + 1) % count, i) for i in range(ends)]),
            ],
            axis=dim,
        )
    return cells


def passed_along(block, axis, distance):
    devices = range(lax.axis_size(axis))
    route = [(i - distance, i) for i in devices if i - distance in devices]
    return lax.ppermute(block, axis, route)


def statistics(values, frame_mask, length, height):
    clip_count, frames, rows_here, cols, chans = values.shape
    sub = chans // GROUPS
    grouped = values.reshape(clip_count, frames, rows_here, cols, GROUPS, sub)
    mask_six = frame_mask[:, :, :, :, :, None]
    count = (length * (height * cols * sub)).astype(jnp.float32)[:, None]
    total = lax.psum(jnp.sum(grouped * mask_six, axis=(1, 2, 3, 5)), "rows")
    mean = total / count
    centered = grouped - mean[:, None, None, None, :, None]
    spread = lax.psum(jnp.sum(centered * centered * mask_six, axis=(1, 2, 3, 5)), "rows")
    var = spread / count
    rstd = lax.rsqrt(var + eps)
    mean_chan = jnp.repeat(mean, sub, axis=-1)[:, None, None, None, :]
    rstd_chan = jnp.repeat(rstd, sub, axis=-1)[:, None, None, None, :]
    return (mean_chan, rstd_chan)


def block(current, length, weight, gain, shift, bias, height):
    clip_count, frames, rows_here, cols, chans = current.shape
    values = current.astype(jnp.float32)
    frame_mask = (jnp.arange(frames)[None, :] < length[:, None]).astype(jnp.float32)[
        :, :, None, None, None
    ]
    mean_chan, rstd_chan = statistics(values, frame_mask, length, height)
    hidden = jax.nn.silu((values - mean_chan) * rstd_chan * gain + shift).astype(jnp.bfloat16)
    extended = extended_2(hidden, (("rows", 2),), 1)
    padded = jnp.pad(extended, ((0, 0), (0, 0), (0, 0), (1, 1), (0, 0)))
    padded = jnp.concatenate([padded[:, :1], padded[:, :1], padded], axis=1)
    pieces = []
    for tap_t in range(3):
        for tap_h in range(3):
            for tap_w in range(3):
                pieces.append(
                    padded[
                        :,
                        tap_t : tap_t + frames,
                        tap_h : tap_h + rows_here,
                        tap_w : tap_w + cols,
                        :,
                    ]
                )
    patches = jnp.concatenate(pieces, axis=-1).reshape(-1, 27 * chans)
    conv = jnp.dot(patches, weight, preferred_element_type=jnp.float32).reshape(values.shape)
    result = ((values + conv + bias) * frame_mask).astype(jnp.bfloat16)
    return (result, patches, frame_mask.astype(jnp.bfloat16))


def relay(clips, lengths, conv_weight, norm_gain, norm_shift, conv_bias, cotangent):
    segments = lax.axis_size("segment")
    segment_id = lax.axis_index("segment")
    micro = clips.shape[0]
    frames = clips.shape[2]
    cols = clips.shape[4]
    chans = clips.shape[5]
    height = clips.shape[3] * lax.axis_size("rows")
    weight = conv_weight[0]
    gain = norm_gain[0]
    shift = norm_shift[0]
    bias = conv_bias[0]
    cot_all = cotangent[0]
    total_cells = micro * clips.shape[1] * lax.axis_size("dp") * frames * height * cols
    factor = 1.0 / math.sqrt(total_cells)

    def tick(step, carry):
        arrived, stash, grads = carry
        which = step - segment_id
        valid = (which >= 0) & (which < micro)
        slot = jnp.clip(which, 0, micro - 1)
        fresh = lax.dynamic_index_in_dim(
            clips, jnp.clip(step, 0, micro - 1).astype(jnp.int32), 0, keepdims=False
        )
        current = jnp.where(segment_id == 0, fresh, arrived)
        length = lax.dynamic_index_in_dim(lengths, slot, 0, keepdims=False)
        result, patches, mask_five = block(current, length, weight, gain, shift, bias, height)
        cot_now = lax.dynamic_index_in_dim(cot_all, slot, 0, keepdims=False)
        masked = (cot_now * mask_five).reshape(-1, chans)
        term = lax.dot_general(
            patches, masked, (((0,), (0,)), ((), ())), preferred_element_type=jnp.float32
        )
        grads = grads + jnp.where(valid, term, 0.0)
        previous = lax.dynamic_index_in_dim(stash, slot, 0, keepdims=False)
        stash = lax.dynamic_update_index_in_dim(stash, jnp.where(valid, result, previous), slot, 0)
        arrived = passed_along(result, "segment", 1)
        return (arrived, stash, grads)

    start = (
        jnp.zeros(clips.shape[1:], jnp.bfloat16),
        jnp.zeros(clips.shape, jnp.bfloat16),
        jnp.zeros((27 * chans, chans), jnp.float32),
    )
    arrived, stash, grads = lax.fori_loop(0, micro + segments - 1, tick, start)
    grads = lax.psum(grads, ("rows", "dp")) * factor
    return (stash[None], grads[None])


TAPS = 9


def swapped(value, axis, flip):
    return lax.ppermute(value, axis, [(i, i ^ flip) for i in range(lax.axis_size(axis))])


def group_sum(value):
    lane = lax.broadcasted_iota(jnp.int32, value.shape, 1)
    chans = value.shape[1]
    for step in (1, 2):
        after = pltpu.roll(value, chans - step, 1)
        before = pltpu.roll(value, step, 1)
        value = value + jnp.where(lane & step == 0, after, before)
    return value


def normalized(values, length, gain, shift):
    frames = len(values)
    positions, chans = values[0].shape
    mask = [(length > f).astype(jnp.float32) for f in range(frames)]
    count = length * (positions * (chans // GROUPS))

    def masked_sum(arrays):
        parts = [
            jnp.sum(a.reshape(positions // 8, 8, chans), axis=0) * m for a, m in zip(arrays, mask)
        ]
        return group_sum(jnp.sum(sum(parts), axis=0, keepdims=True))

    mean = masked_sum(values) / count
    centered = [v - mean for v in values]
    var = masked_sum([c * c for c in centered]) / count
    rstd = lax.rsqrt(var + eps)
    normed = [c * rstd * gain + shift for c in centered]
    return [v / (1.0 + jnp.exp(-v)) for v in normed]


def taps_of(hidden, cols):
    positions, lanes = hidden.shape
    rows = positions // cols
    zero = jnp.zeros((1, cols, lanes), jnp.float32)
    padded = jnp.concatenate([zero, hidden.reshape(rows, cols, lanes), zero], axis=0)
    col = lax.broadcasted_iota(jnp.int32, padded.shape, 1)
    left = jnp.where(col == 0, 0.0, pltpu.roll(padded, 1, 1))
    right = jnp.where(col == cols - 1, 0.0, pltpu.roll(padded, cols - 1, 1))
    pieces = [
        value[b : b + rows].reshape(positions, lanes).astype(jnp.bfloat16)
        for b in range(3)
        for value in (left, padded, right)
    ]
    return jnp.concatenate(pieces, axis=1)


def convolved(hidden, weight_ref, cols):
    frames = len(hidden)
    chans = hidden[0].shape[1]
    depth = TAPS * chans
    outs = [None] * frames
    for source in range(frames):
        patch = taps_of(hidden[source], cols)
        uses = [(f, a) for f in range(frames) for a in range(3) if max(f + a - 2, 0) == source]
        needed = sorted({a for _, a in uses})
        weight = jnp.concatenate([weight_ref[a * depth : (a + 1) * depth] for a in needed], axis=1)
        product = jnp.dot(patch, weight, preferred_element_type=jnp.float32)
        for f, a in uses:
            at = needed.index(a) * chans
            term = product[:, at : at + chans]
            outs[f] = term if outs[f] is None else outs[f] + term
    return outs


def real_frames(lengths):
    index = lax.broadcasted_iota(jnp.int32, lengths.shape, 1)
    mine = jnp.where(index == lax.axis_index("rows"), lengths[...].astype(jnp.float32), 0.0)
    return jnp.sum(mine, axis=1, keepdims=True)


def split_three(value):
    high = lax.reduce_precision(value, 8, 7)
    rest = value - high
    middle = lax.reduce_precision(rest, 8, 7)
    return jnp.stack([high, middle, rest - middle]).astype(jnp.bfloat16)


def prepare_kernel(lengths, clips, *refs):
    pieces, (arrived, gain, shift, bias, whole, hidden, params) = refs[:3], refs[3:]
    segment, row = lax.axis_index("segment"), lax.axis_index("rows")
    _, frames, span, chans = pieces[0].shape
    for k, piece in enumerate([clips.at[row], *[p.at[0] for p in pieces]]):
        whole[:, pl.ds(pl.multiple_of((row ^ k) * span, span), span), :] = piece[...]
    extra = arrived[arrived.shape[0] - 16 :].astype(jnp.float32)
    sent = [extra[i : i + 1] + extra[i + 3 : i + 4] + extra[i + 6 : i + 7] for i in range(3)]
    own = (gain, shift, bias)
    used = [jnp.where(segment == 0, o[...], s) for o, s in zip(own, sent)]
    values = [whole[f].astype(jnp.float32) for f in range(frames)]
    out = normalized(values, real_frames(lengths), used[0], used[1])
    for f in range(frames):
        hidden[f] = out[f].astype(jnp.bfloat16)
    params[...] = jnp.broadcast_to(used[2], params.shape)


def first_kernel(
    cols, lengths, whole, hidden, own_weight, arrived, other, params, gain, shift, *refs
):
    (mine, near, far, middle, after, weight) = refs
    slices = [mine, near, far.at[0], far.at[1]]
    segment, part = lax.axis_index("segment"), lax.axis_index("dp")
    frames, positions, chans = whole.shape
    real = real_frames(lengths)
    half = own_weight.shape[0] // 2
    core = part & 1

    @pl.when(segment == 0)
    def _():
        weight[...] = own_weight[...]

    @pl.when(segment != 0)
    def _():
        at = pl.multiple_of(core * half, 16)
        weight[pl.ds(at, half)] = arrived[:half]
        at = pl.multiple_of((1 - core) * half, 16)
        weight[pl.ds(at, half)] = other[:half]

    before = [hidden[f].astype(jnp.float32) for f in range(frames)]
    outs = convolved(before, weight, cols)
    bias = params[0:1]
    values = []
    for f in range(frames):
        out = (whole[f].astype(jnp.float32) + outs[f] + bias) * (real > f).astype(jnp.float32)
        middle[f] = out.astype(jnp.bfloat16)
        values.append(middle[f].astype(jnp.float32))
    out = normalized(values, real, gain[...], shift[...])
    out = [o.astype(jnp.bfloat16).astype(jnp.float32) for o in out]
    for f in range(frames):
        after[f] = out[f].astype(jnp.bfloat16)
    chosen = [jnp.where(segment == 0, b, o) for b, o in zip(before, out)]
    quarter = chans // 4
    group = lax.broadcasted_iota(jnp.int32, (positions, chans), 1) // quarter
    for k in range(4):
        packed = None
        for f in range(frames):
            moved = pltpu.roll(chosen[f], ((f - (part ^ k)) & 3) * quarter, 1)
            packed = moved if packed is None else jnp.where(group == f, moved, packed)
        slices[k][...] = packed.astype(jnp.bfloat16)


def second_kernel(cols, lengths, middle, after, weight, bias, *refs):
    mine, outer, inner, stash = refs
    pieces = [mine, outer.at[0], inner, outer.at[1]]
    segment, row = lax.axis_index("segment"), lax.axis_index("rows")
    frames, positions, chans = middle.shape
    span = positions // 4
    real = real_frames(lengths)

    @pl.when(segment == 0)
    def _():
        stash[...] = middle[...]

    @pl.when(segment != 0)
    def _():
        outs = convolved([after[f].astype(jnp.float32) for f in range(frames)], weight, cols)
        for f in range(frames):
            out = middle[f].astype(jnp.float32) + outs[f] + bias[...]
            stash[f] = (out * (real > f).astype(jnp.float32)).astype(jnp.bfloat16)

    for k, piece in enumerate(pieces):
        piece[...] = stash[:, pl.ds(pl.multiple_of((row ^ k) * span, span), span), :]


def cotangent_kernel(lengths, cotangent, *refs):
    pieces, (turned, whole) = refs[:3], refs[3:]
    row = lax.axis_index("rows")
    _, frames, span, chans = pieces[0].shape
    real = real_frames(lengths)
    for k, piece in enumerate([cotangent.at[row], *[p.at[1] for p in pieces]]):
        whole[:, pl.ds(pl.multiple_of((row ^ k) * span, span), span), :] = piece[...]
    for f in range(frames):
        value = whole[f].astype(jnp.float32) * (real > f).astype(jnp.float32)
        turned[f * chans : (f + 1) * chans] = value.T.astype(jnp.bfloat16)


def gradient_kernel(cols, *refs):
    slices, cots, (send, keep, grad) = refs[:4], refs[4:8], refs[8:]
    row = lax.axis_index("rows")
    chans = slices[0].shape[1]
    quarter = chans // 4
    patches = jnp.concatenate([taps_of(s[...].astype(jnp.float32), cols) for s in slices], axis=0)
    left = jnp.concatenate([c[...] for c in cots], axis=1)
    product = jnp.dot(left, patches, preferred_element_type=jnp.float32)
    group = lax.broadcasted_iota(jnp.int32, (chans, chans), 1) // quarter
    for tap in range(TAPS):
        total = None
        for f in range(4):
            value = product[f * chans : (f + 1) * chans, tap * chans : (tap + 1) * chans]
            moved = None
            for a in range(3):
                by = (a - max(f + a - 2, 0)) * quarter % chans
                turned = pltpu.roll(value, by, 1) if by else value
                moved = turned if moved is None else jnp.where(group == a, turned, moved)
            total = moved if total is None else total + moved
        total = total.T
        for a in range(3):
            grad[a * TAPS + tap] = total[a * quarter : (a + 1) * quarter]
    low = row & 1
    part = quarter // 2
    there = grad[:, pl.ds(pl.multiple_of((1 - low) * part, part), part), :]
    send[...] = there.reshape(send.shape).astype(jnp.bfloat16)
    keep[...] = grad[:, pl.ds(pl.multiple_of(low * part, part), part), :].reshape(keep.shape)


def halving_kernel(keep, got, send, kept, total):
    high = lax.axis_index("rows") >> 1
    value = keep[...] + got[...].astype(jnp.float32)
    total[...] = value.reshape(total.shape)
    there = total[:, pl.ds(pl.multiple_of((1 - high) * 8, 8), 8), :]
    send[...] = there.reshape(send.shape).astype(jnp.bfloat16)
    kept[...] = total[:, pl.ds(pl.multiple_of(high * 8, 8), 8), :].reshape(kept.shape)


def finish_kernel(upper, lower, *refs):
    pieces, (grads, stash) = refs[:4], refs[4:]
    row, part = lax.axis_index("rows"), lax.axis_index("dp")
    taps, chans, _ = grads.shape
    for i, source in enumerate((upper, lower)):
        for j in range(2):
            for k in range(2):
                for l in range(2):
                    at = (part ^ (i + 2 * j)) * 32 + ((row & 1) ^ k) * 16 + ((row >> 1) ^ l) * 8
                    value = source[j, k, l].astype(jnp.float32).reshape(taps, 8, chans)
                    grads[:, pl.ds(pl.multiple_of(at, 8), 8), :] = value
    for k, piece in enumerate(pieces):
        stash[pl.ds(row ^ k, 1)] = piece[...][None]


def whole_clips(clips, lengths, conv_weight, norm_gain, norm_shift, conv_bias, cotangent):
    row = lax.axis_index("rows")
    part = lax.axis_index("dp")
    micro, _, frames, rows_here, cols, chans = clips.shape
    span = rows_here * cols
    positions = span * micro
    total_cells = micro * lax.axis_size("dp") * frames * positions
    factor = 1.0 / math.sqrt(total_cells)
    core = part & 1
    weight = conv_weight[0]
    half = weight.shape[0] // 2
    bf16, f32 = jnp.bfloat16, jnp.float32
    shape = jax.ShapeDtypeStruct
    vmem = pl.BlockSpec(memory_space=pltpu.VMEM)
    params = pltpu.CompilerParams(vmem_limit_bytes=48 * 1024 * 1024)

    def call(kernel, outs, scratch, args):
        return pl.pallas_call(
            kernel,
            out_shape=outs,
            in_specs=[vmem] * len(args),
            out_specs=[vmem] * len(outs),
            scratch_shapes=scratch,
            compiler_params=params,
        )(*args)

    clip_like = shape((frames, positions, chans), bf16)
    piece_like = shape((frames, span, chans), bf16)

    clips_here = clips.reshape(micro, frames, span, chans)
    cot_here = cotangent.reshape(micro, frames, span, chans)
    lengths = jnp.transpose(lengths)

    extras = split_three(jnp.concatenate([norm_gain, norm_shift, conv_bias])).reshape(9, chans)
    extras = jnp.pad(extras, ((0, 7), (0, 0)))
    mine = lax.dynamic_slice_in_dim(weight, core * half, half)
    arrived = lax.ppermute(jnp.concatenate([mine, extras]), "segment", [(0, 1)])

    pieces = []
    for k in range(1, micro):
        both = [lax.dynamic_index_in_dim(v, row ^ k, 0) for v in (clips_here, cot_here)]
        pieces.append(swapped(jnp.concatenate(both), "rows", k))

    pieces, arrived = lax.optimization_barrier((pieces, arrived))
    other = swapped(arrived, "dp", 1)
    whole, hidden, bias0 = call(
        prepare_kernel,
        [clip_like, clip_like, shape((8, chans), f32)],
        [],
        [lengths, clips_here, *pieces, arrived, norm_gain, norm_shift, conv_bias],
    )

    (turned,) = call(
        cotangent_kernel,
        [shape((frames * chans, positions), bf16)],
        [pltpu.VMEM((frames, positions, chans), bf16)],
        [lengths, cot_here, *pieces],
    )
    cots = {0: turned, 2: swapped(turned, "dp", 2)}
    cots[1] = swapped(turned, "dp", 1)

    slice_like = shape((positions, chans), bf16)
    mine, near, far, middle, after = call(
        functools.partial(first_kernel, cols),
        [slice_like, slice_like, shape((2, positions, chans), bf16), clip_like, clip_like],
        [pltpu.VMEM(weight.shape, bf16)],
        [lengths, whole, hidden, weight, arrived, other, bias0, norm_gain, norm_shift],
    )
    far = swapped(far, "dp", 2)

    own_piece, outer, inner = call(
        functools.partial(second_kernel, cols),
        [piece_like, shape((2, *piece_like.shape), bf16), piece_like],
        [pltpu.VMEM((frames, positions, chans), bf16)],
        [lengths, middle, after, weight, conv_bias],
    )
    far, cots[2], outer = lax.optimization_barrier((far, cots[2], outer))
    cots[3] = swapped(cots[2], "dp", 1)
    near = swapped(jnp.stack([near, far[1]]), "dp", 1)
    outer = swapped(outer, "rows", 1)
    held = [mine, near[0], far[0], near[1]]

    quarter = chans // 4
    rows_sent = 27 * quarter // 2
    send, keep = call(
        functools.partial(gradient_kernel, cols),
        [shape((rows_sent, chans), bf16), shape((rows_sent, chans), f32)],
        [pltpu.VMEM((27, quarter, chans), f32)],
        [*held, *[cots[k] for k in range(4)]],
    )
    rows_kept = rows_sent // 2
    send, keep = call(
        halving_kernel,
        [shape((rows_kept, chans), bf16), shape((rows_kept, chans), f32)],
        [pltpu.VMEM((27, quarter // 2, chans), f32)],
        [keep, swapped(send, "rows", 1)],
    )
    total = (keep + swapped(send, "rows", 2).astype(f32)) * factor
    total = total.astype(bf16)
    total = jnp.stack([total, swapped(total, "rows", 2)])
    total, inner, outer = lax.optimization_barrier((total, inner, outer))
    inner = swapped(jnp.stack([inner, outer[1]]), "rows", 2)
    total = jnp.stack([total, swapped(total, "rows", 1)])
    got, inner = lax.optimization_barrier((swapped(total, "dp", 2), inner))
    total = jnp.stack([total, got])
    grads, stash = call(
        finish_kernel,
        [shape((27, chans, chans), f32), shape((micro, frames, span, chans), bf16)],
        [],
        [total, swapped(total, "dp", 1), own_piece, outer[0], inner[0], inner[1]],
    )
    return (stash.reshape((1,) + clips.shape), grads.reshape(1, 27 * chans, chans))


def per_device(clips, lengths, conv_weight, norm_gain, norm_shift, conv_bias, cotangent):
    sizes = [lax.axis_size(axis) for axis in ("segment", "rows", "dp")]
    fits = sizes == [2, 4, 4] and clips.shape[0] == 4 and clips.shape[1] == 1
    plan = whole_clips if fits and clips.shape[5] == 128 else relay
    return plan(clips, lengths, conv_weight, norm_gain, norm_shift, conv_bias, cotangent)


def solution(mesh):
    in_specs = (
        P(None, "dp", None, "rows", None, None),
        P(None, "dp"),
        P("segment", None, None),
        P("segment", None),
        P("segment", None),
        P("segment", None),
        P("segment", None, "dp", None, "rows", None, None),
    )
    out_specs = (P("segment", None, "dp", None, "rows", None, None), P("segment", None, None))
    return jax.shard_map(
        per_device, mesh=mesh, in_specs=in_specs, out_specs=out_specs, check_vma=False
    )
```

```python
import functools
import math

import jax
import jax.numpy as jnp
from jax import lax
from jax.experimental import pallas as pl
from jax.experimental.pallas import tpu as pltpu
from jax.sharding import PartitionSpec as P

GROUPS = 32


eps = 1e-06


def extended_2(cells, sides, width):
    for axis, dim in sides:
        count = lax.axis_size(axis)
        ends = count - 1
        head = lax.slice_in_dim(cells, 0, width, axis=dim)
        tail = lax.slice_in_dim(cells, cells.shape[dim] - width, cells.shape[dim], axis=dim)
        cells = jnp.concatenate(
            [
                lax.ppermute(tail, axis, [(i, (i + 1) % count) for i in range(ends)]),
                cells,
                lax.ppermute(head, axis, [((i + 1) % count, i) for i in range(ends)]),
            ],
            axis=dim,
        )
    return cells


def passed_along(block, axis, distance):
    devices = range(lax.axis_size(axis))
    route = [(i - distance, i) for i in devices if i - distance in devices]
    return lax.ppermute(block, axis, route)


def statistics(values, frame_mask, length, height):
    clip_count, frames, rows_here, cols, chans = values.shape
    sub = chans // GROUPS
    grouped = values.reshape(clip_count, frames, rows_here, cols, GROUPS, sub)
    mask_six = frame_mask[:, :, :, :, :, None]
    count = (length * (height * cols * sub)).astype(jnp.float32)[:, None]
    total = lax.psum(jnp.sum(grouped * mask_six, axis=(1, 2, 3, 5)), "rows")
    mean = total / count
    centered = grouped - mean[:, None, None, None, :, None]
    spread = lax.psum(jnp.sum(centered * centered * mask_six, axis=(1, 2, 3, 5)), "rows")
    var = spread / count
    rstd = lax.rsqrt(var + eps)
    mean_chan = jnp.repeat(mean, sub, axis=-1)[:, None, None, None, :]
    rstd_chan = jnp.repeat(rstd, sub, axis=-1)[:, None, None, None, :]
    return (mean_chan, rstd_chan)


def block(current, length, weight, gain, shift, bias, height):
    clip_count, frames, rows_here, cols, chans = current.shape
    values = current.astype(jnp.float32)
    frame_mask = (jnp.arange(frames)[None, :] < length[:, None]).astype(jnp.float32)[
        :, :, None, None, None
    ]
    mean_chan, rstd_chan = statistics(values, frame_mask, length, height)
    hidden = jax.nn.silu((values - mean_chan) * rstd_chan * gain + shift).astype(jnp.bfloat16)
    extended = extended_2(hidden, (("rows", 2),), 1)
    padded = jnp.pad(extended, ((0, 0), (0, 0), (0, 0), (1, 1), (0, 0)))
    padded = jnp.concatenate([padded[:, :1], padded[:, :1], padded], axis=1)
    pieces = []
    for tap_t in range(3):
        for tap_h in range(3):
            for tap_w in range(3):
                pieces.append(
                    padded[
                        :,
                        tap_t : tap_t + frames,
                        tap_h : tap_h + rows_here,
                        tap_w : tap_w + cols,
                        :,
                    ]
                )
    patches = jnp.concatenate(pieces, axis=-1).reshape(-1, 27 * chans)
    conv = jnp.dot(patches, weight, preferred_element_type=jnp.float32).reshape(values.shape)
    result = ((values + conv + bias) * frame_mask).astype(jnp.bfloat16)
    return (result, patches, frame_mask.astype(jnp.bfloat16))


def relay(clips, lengths, conv_weight, norm_gain, norm_shift, conv_bias, cotangent):
    segments = lax.axis_size("segment")
    segment_id = lax.axis_index("segment")
    micro = clips.shape[0]
    frames = clips.shape[2]
    cols = clips.shape[4]
    chans = clips.shape[5]
    height = clips.shape[3] * lax.axis_size("rows")
    weight = conv_weight[0]
    gain = norm_gain[0]
    shift = norm_shift[0]
    bias = conv_bias[0]
    cot_all = cotangent[0]
    total_cells = micro * clips.shape[1] * lax.axis_size("dp") * frames * height * cols
    factor = 1.0 / math.sqrt(total_cells)

    def tick(step, carry):
        arrived, stash, grads = carry
        which = step - segment_id
        valid = (which >= 0) & (which < micro)
        slot = jnp.clip(which, 0, micro - 1)
        fresh = lax.dynamic_index_in_dim(
            clips, jnp.clip(step, 0, micro - 1).astype(jnp.int32), 0, keepdims=False
        )
        current = jnp.where(segment_id == 0, fresh, arrived)
        length = lax.dynamic_index_in_dim(lengths, slot, 0, keepdims=False)
        result, patches, mask_five = block(current, length, weight, gain, shift, bias, height)
        cot_now = lax.dynamic_index_in_dim(cot_all, slot, 0, keepdims=False)
        masked = (cot_now * mask_five).reshape(-1, chans)
        term = lax.dot_general(
            patches, masked, (((0,), (0,)), ((), ())), preferred_element_type=jnp.float32
        )
        grads = grads + jnp.where(valid, term, 0.0)
        previous = lax.dynamic_index_in_dim(stash, slot, 0, keepdims=False)
        stash = lax.dynamic_update_index_in_dim(stash, jnp.where(valid, result, previous), slot, 0)
        arrived = passed_along(result, "segment", 1)
        return (arrived, stash, grads)

    start = (
        jnp.zeros(clips.shape[1:], jnp.bfloat16),
        jnp.zeros(clips.shape, jnp.bfloat16),
        jnp.zeros((27 * chans, chans), jnp.float32),
    )
    arrived, stash, grads = lax.fori_loop(0, micro + segments - 1, tick, start)
    grads = lax.psum(grads, ("rows", "dp")) * factor
    return (stash[None], grads[None])


TAPS = 9


def swapped(value, axis, flip):
    return lax.ppermute(value, axis, [(i, i ^ flip) for i in range(lax.axis_size(axis))])


def group_sum(value):
    lane = lax.broadcasted_iota(jnp.int32, value.shape, 1)
    chans = value.shape[1]
    for step in (1, 2):
        after = pltpu.roll(value, chans - step, 1)
        before = pltpu.roll(value, step, 1)
        value = value + jnp.where(lane & step == 0, after, before)
    return value


def normalized(values, length, gain, shift):
    frames = len(values)
    positions, chans = values[0].shape
    mask = [(length > f).astype(jnp.float32) for f in range(frames)]
    count = length * (positions * (chans // GROUPS))

    def masked_sum(arrays):
        parts = [
            jnp.sum(a.reshape(positions // 8, 8, chans), axis=0) * m for a, m in zip(arrays, mask)
        ]
        return group_sum(jnp.sum(sum(parts), axis=0, keepdims=True))

    mean = masked_sum(values) / count
    centered = [v - mean for v in values]
    var = masked_sum([c * c for c in centered]) / count
    rstd = lax.rsqrt(var + eps)
    normed = [c * rstd * gain + shift for c in centered]
    return [v / (1.0 + jnp.exp(-v)) for v in normed]


def taps_of(hidden, cols):
    positions, lanes = hidden.shape
    rows = positions // cols
    zero = jnp.zeros((1, cols, lanes), jnp.float32)
    padded = jnp.concatenate([zero, hidden.reshape(rows, cols, lanes), zero], axis=0)
    col = lax.broadcasted_iota(jnp.int32, padded.shape, 1)
    left = jnp.where(col == 0, 0.0, pltpu.roll(padded, 1, 1))
    right = jnp.where(col == cols - 1, 0.0, pltpu.roll(padded, cols - 1, 1))
    pieces = [
        value[b : b + rows].reshape(positions, lanes).astype(jnp.bfloat16)
        for b in range(3)
        for value in (left, padded, right)
    ]
    return jnp.concatenate(pieces, axis=1)


def convolved(hidden, weight_ref, cols):
    frames = len(hidden)
    chans = hidden[0].shape[1]
    depth = TAPS * chans
    outs = [None] * frames
    for source in range(frames):
        patch = taps_of(hidden[source], cols)
        uses = [(f, a) for f in range(frames) for a in range(3) if max(f + a - 2, 0) == source]
        needed = sorted({a for _, a in uses})
        weight = jnp.concatenate([weight_ref[a * depth : (a + 1) * depth] for a in needed], axis=1)
        product = jnp.dot(patch, weight, preferred_element_type=jnp.float32)
        for f, a in uses:
            at = needed.index(a) * chans
            term = product[:, at : at + chans]
            outs[f] = term if outs[f] is None else outs[f] + term
    return outs


def real_frames(lengths):
    index = lax.broadcasted_iota(jnp.int32, lengths.shape, 1)
    mine = jnp.where(index == lax.axis_index("rows"), lengths[...].astype(jnp.float32), 0.0)
    return jnp.sum(mine, axis=1, keepdims=True)


def split_three(value):
    high = lax.reduce_precision(value, 8, 7)
    rest = value - high
    middle = lax.reduce_precision(rest, 8, 7)
    return jnp.stack([high, middle, rest - middle]).astype(jnp.bfloat16)


def prepare_kernel(lengths, clips, *refs):
    pieces, (arrived, gain, shift, bias, whole, hidden, params) = refs[:3], refs[3:]
    segment, row = lax.axis_index("segment"), lax.axis_index("rows")
    _, frames, span, chans = pieces[0].shape
    for k, piece in enumerate([clips.at[row], *[p.at[0] for p in pieces]]):
        whole[:, pl.ds(pl.multiple_of((row ^ k) * span, span), span), :] = piece[...]
    extra = arrived[arrived.shape[0] - 16 :].astype(jnp.float32)
    sent = [extra[i : i + 1] + extra[i + 3 : i + 4] + extra[i + 6 : i + 7] for i in range(3)]
    own = (gain, shift, bias)
    used = [jnp.where(segment == 0, o[...], s) for o, s in zip(own, sent)]
    values = [whole[f].astype(jnp.float32) for f in range(frames)]
    out = normalized(values, real_frames(lengths), used[0], used[1])
    for f in range(frames):
        hidden[f] = out[f].astype(jnp.bfloat16)
    params[...] = jnp.broadcast_to(used[2], params.shape)


def first_kernel(
    cols, lengths, whole, hidden, own_weight, arrived, other, params, gain, shift, *refs
):
    (mine, near, far, middle, after, weight) = refs
    slices = [mine, near, far.at[0], far.at[1]]
    segment, part = lax.axis_index("segment"), lax.axis_index("dp")
    frames, positions, chans = whole.shape
    real = real_frames(lengths)
    half = own_weight.shape[0] // 2
    core = part & 1

    @pl.when(segment == 0)
    def _():
        weight[...] = own_weight[...]

    @pl.when(segment != 0)
    def _():
        at = pl.multiple_of(core * half, 16)
        weight[pl.ds(at, half)] = arrived[:half]
        at = pl.multiple_of((1 - core) * half, 16)
        weight[pl.ds(at, half)] = other[:half]

    before = [hidden[f].astype(jnp.float32) for f in range(frames)]
    outs = convolved(before, weight, cols)
    bias = params[0:1]
    values = []
    for f in range(frames):
        out = (whole[f].astype(jnp.float32) + outs[f] + bias) * (real > f).astype(jnp.float32)
        middle[f] = out.astype(jnp.bfloat16)
        values.append(middle[f].astype(jnp.float32))
    out = normalized(values, real, gain[...], shift[...])
    out = [o.astype(jnp.bfloat16).astype(jnp.float32) for o in out]
    for f in range(frames):
        after[f] = out[f].astype(jnp.bfloat16)
    chosen = [jnp.where(segment == 0, b, o) for b, o in zip(before, out)]
    quarter = chans // 4
    group = lax.broadcasted_iota(jnp.int32, (positions, chans), 1) // quarter
    for k in range(4):
        packed = None
        for f in range(frames):
            moved = pltpu.roll(chosen[f], ((f - (part ^ k)) & 3) * quarter, 1)
            packed = moved if packed is None else jnp.where(group == f, moved, packed)
        slices[k][...] = packed.astype(jnp.bfloat16)


def second_kernel(cols, lengths, middle, after, weight, bias, *refs):
    mine, outer, inner, stash = refs
    pieces = [mine, outer.at[0], inner, outer.at[1]]
    segment, row = lax.axis_index("segment"), lax.axis_index("rows")
    frames, positions, chans = middle.shape
    span = positions // 4
    real = real_frames(lengths)

    @pl.when(segment == 0)
    def _():
        stash[...] = middle[...]

    @pl.when(segment != 0)
    def _():
        outs = convolved([after[f].astype(jnp.float32) for f in range(frames)], weight, cols)
        for f in range(frames):
            out = middle[f].astype(jnp.float32) + outs[f] + bias[...]
            stash[f] = (out * (real > f).astype(jnp.float32)).astype(jnp.bfloat16)

    for k, piece in enumerate(pieces):
        piece[...] = stash[:, pl.ds(pl.multiple_of((row ^ k) * span, span), span), :]


def cotangent_kernel(early, late, turned, whole):
    row = lax.axis_index("rows")
    _, frames, span, chans = early.shape
    for k, piece in enumerate([early.at[0], early.at[1], late.at[0], late.at[1]]):
        whole[:, pl.ds(pl.multiple_of((row ^ k) * span, span), span), :] = piece[...]
    for f in range(frames):
        turned[f * chans : (f + 1) * chans] = whole[f].astype(jnp.float32).T.astype(jnp.bfloat16)


def gradient_kernel(cols, *refs):
    slices, cots, (send, keep, grad) = refs[:4], refs[4:8], refs[8:]
    row = lax.axis_index("rows")
    chans = slices[0].shape[1]
    quarter = chans // 4
    patches = jnp.concatenate([taps_of(s[...].astype(jnp.float32), cols) for s in slices], axis=0)
    left = jnp.concatenate([c[...] for c in cots], axis=1)
    product = jnp.dot(left, patches, preferred_element_type=jnp.float32)
    group = lax.broadcasted_iota(jnp.int32, (chans, chans), 1) // quarter
    for tap in range(TAPS):
        total = None
        for f in range(4):
            value = product[f * chans : (f + 1) * chans, tap * chans : (tap + 1) * chans]
            moved = None
            for a in range(3):
                by = (a - max(f + a - 2, 0)) * quarter % chans
                turned = pltpu.roll(value, by, 1) if by else value
                moved = turned if moved is None else jnp.where(group == a, turned, moved)
            total = moved if total is None else total + moved
        total = total.T
        for a in range(3):
            grad[a * TAPS + tap] = total[a * quarter : (a + 1) * quarter]
    low = row & 1
    part = quarter // 2
    there = grad[:, pl.ds(pl.multiple_of((1 - low) * part, part), part), :]
    send[...] = there.reshape(send.shape).astype(jnp.bfloat16)
    keep[...] = grad[:, pl.ds(pl.multiple_of(low * part, part), part), :].reshape(keep.shape)


def finish_kernel(total, lower, across, last, beside, last_beside, *refs):
    pieces, (grads, stash) = refs[:4], refs[4:]
    row, part = lax.axis_index("rows"), lax.axis_index("dp")
    taps = grads.shape[0]
    sources = (total, lower, across, last)
    sources += (beside.at[0], beside.at[1], beside.at[2], last_beside)
    for n, source in enumerate(sources):
        i, j, k = n >> 2, n >> 1 & 1, n & 1
        at = (part ^ (i + 2 * j)) * 32 + ((row & 1) ^ k) * 16
        value = source[...].astype(jnp.float32).reshape(taps, 16, grads.shape[2])
        grads[:, pl.ds(pl.multiple_of(at, 16), 16), :] = value
    for k, piece in enumerate(pieces):
        stash[pl.ds(row ^ k, 1)] = piece[...][None]


def whole_clips(clips, lengths, conv_weight, norm_gain, norm_shift, conv_bias, cotangent):
    row = lax.axis_index("rows")
    part = lax.axis_index("dp")
    micro, _, frames, rows_here, cols, chans = clips.shape
    span = rows_here * cols
    positions = span * micro
    total_cells = micro * lax.axis_size("dp") * frames * positions
    factor = 1.0 / math.sqrt(total_cells)
    core = part & 1
    weight = conv_weight[0]
    half = weight.shape[0] // 2
    bf16, f32 = jnp.bfloat16, jnp.float32
    shape = jax.ShapeDtypeStruct
    vmem = pl.BlockSpec(memory_space=pltpu.VMEM)
    params = pltpu.CompilerParams(vmem_limit_bytes=48 * 1024 * 1024)

    def call(kernel, outs, scratch, args):
        return pl.pallas_call(
            kernel,
            out_shape=outs,
            in_specs=[vmem] * len(args),
            out_specs=[vmem] * len(outs),
            scratch_shapes=scratch,
            compiler_params=params,
        )(*args)

    clip_like = shape((frames, positions, chans), bf16)
    piece_like = shape((frames, span, chans), bf16)

    clips_here = clips.reshape(micro, frames, span, chans)
    cot_here = cotangent.reshape(micro, frames, span, chans)
    lengths = jnp.transpose(lengths)

    extras = split_three(jnp.concatenate([norm_gain, norm_shift, conv_bias])).reshape(9, chans)
    extras = jnp.pad(extras, ((0, 7), (0, 0)))
    mine = lax.dynamic_slice_in_dim(weight, core * half, half)
    arrived = lax.ppermute(jnp.concatenate([mine, extras]), "segment", [(0, 1)])

    def spread(pieces):
        return [swapped(piece, "rows", k + 1) for k, piece in enumerate(pieces)]

    pieces = []
    for k in range(1, micro):
        both = [lax.dynamic_index_in_dim(v, row ^ k, 0) for v in (clips_here, cot_here)]
        pieces.append(jnp.concatenate(both))
    pieces = spread(pieces)

    length = lax.dynamic_index_in_dim(lengths[0], row, 0, keepdims=False)
    mask = (jnp.arange(frames) < length).astype(bf16)[:, None, None]
    own_cot = lax.dynamic_index_in_dim(cot_here, row, 0, keepdims=False)
    early = jnp.stack([own_cot, pieces[0][1]]) * mask
    late = jnp.stack([pieces[1][1], pieces[2][1]]) * mask
    early_across = swapped(early, "dp", 2)
    pieces, late, arrived = lax.optimization_barrier((pieces, late, arrived))
    late_across = swapped(late, "dp", 2)

    def turned(first, second):
        return call(
            cotangent_kernel,
            [shape((frames * chans, positions), bf16)],
            [pltpu.VMEM((frames, positions, chans), bf16)],
            [first, second],
        )[0]

    cots = {0: turned(early, late)}
    cots[1] = swapped(cots[0], "dp", 1)

    other = swapped(arrived, "dp", 1)
    whole, hidden, bias0 = call(
        prepare_kernel,
        [clip_like, clip_like, shape((8, chans), f32)],
        [],
        [lengths, clips_here, *pieces, arrived, norm_gain, norm_shift, conv_bias],
    )

    slice_like = shape((positions, chans), bf16)
    mine, near, far, middle, after = call(
        functools.partial(first_kernel, cols),
        [slice_like, slice_like, shape((2, positions, chans), bf16), clip_like, clip_like],
        [pltpu.VMEM(weight.shape, bf16)],
        [lengths, whole, hidden, weight, arrived, other, bias0, norm_gain, norm_shift],
    )
    far = swapped(far, "dp", 2)

    own_piece, outer, inner = call(
        functools.partial(second_kernel, cols),
        [piece_like, shape((2, *piece_like.shape), bf16), piece_like],
        [pltpu.VMEM((frames, positions, chans), bf16)],
        [lengths, middle, after, weight, conv_bias],
    )
    far, early_across, late_across = lax.optimization_barrier((far, early_across, late_across))
    cots[2] = turned(early_across, late_across)
    cots[3] = swapped(cots[2], "dp", 1)
    near = swapped(jnp.stack([near, far[1]]), "dp", 1)
    outer = swapped(outer, "rows", 1)
    inner = swapped(jnp.stack([inner, outer[1]]), "rows", 2)
    held = [mine, near[0], far[0], near[1]]

    quarter = chans // 4
    rows_sent = 27 * quarter // 2
    send, keep = call(
        functools.partial(gradient_kernel, cols),
        [shape((rows_sent, chans), bf16), shape((rows_sent, chans), f32)],
        [pltpu.VMEM((27, quarter, chans), f32)],
        [*held, *[cots[k] for k in range(4)]],
    )
    got, inner = lax.optimization_barrier((swapped(send, "rows", 1), inner))
    total = (keep + got.astype(f32)).astype(bf16)
    total = (total.astype(f32) + swapped(total, "rows", 2).astype(f32)) * factor
    total = total.astype(bf16)
    lower = swapped(total, "rows", 1)
    across = swapped(total, "dp", 2)
    last = swapped(lower, "dp", 2)
    beside = swapped(jnp.stack([total, lower, across]), "dp", 1)
    grads, stash = call(
        finish_kernel,
        [shape((27, chans, chans), f32), shape((micro, frames, span, chans), bf16)],
        [],
        [
            *[total, lower, across, last, beside, swapped(last, "dp", 1)],
            *[own_piece, outer[0], inner[0], inner[1]],
        ],
    )
    return (stash.reshape((1,) + clips.shape), grads.reshape(1, 27 * chans, chans))


def per_device(clips, lengths, conv_weight, norm_gain, norm_shift, conv_bias, cotangent):
    sizes = [lax.axis_size(axis) for axis in ("segment", "rows", "dp")]
    fits = sizes == [2, 4, 4] and clips.shape[0] == 4 and clips.shape[1] == 1
    plan = whole_clips if fits and clips.shape[5] == 128 else relay
    return plan(clips, lengths, conv_weight, norm_gain, norm_shift, conv_bias, cotangent)


def solution(mesh):
    in_specs = (
        P(None, "dp", None, "rows", None, None),
        P(None, "dp"),
        P("segment", None, None),
        P("segment", None),
        P("segment", None),
        P("segment", None),
        P("segment", None, "dp", None, "rows", None, None),
    )
    out_specs = (P("segment", None, "dp", None, "rows", None, None), P("segment", None, None))
    return jax.shard_map(
        per_device, mesh=mesh, in_specs=in_specs, out_specs=out_specs, check_vma=False
    )
```

```python
import functools
import math

import jax
import jax.numpy as jnp
from jax import lax
from jax.experimental import pallas as pl
from jax.experimental.pallas import tpu as pltpu
from jax.sharding import PartitionSpec as P

GROUPS = 32


eps = 1e-06


def extended_2(cells, sides, width):
    for axis, dim in sides:
        count = lax.axis_size(axis)
        ends = count - 1
        head = lax.slice_in_dim(cells, 0, width, axis=dim)
        tail = lax.slice_in_dim(cells, cells.shape[dim] - width, cells.shape[dim], axis=dim)
        cells = jnp.concatenate(
            [
                lax.ppermute(tail, axis, [(i, (i + 1) % count) for i in range(ends)]),
                cells,
                lax.ppermute(head, axis, [((i + 1) % count, i) for i in range(ends)]),
            ],
            axis=dim,
        )
    return cells


def passed_along(block, axis, distance):
    devices = range(lax.axis_size(axis))
    route = [(i - distance, i) for i in devices if i - distance in devices]
    return lax.ppermute(block, axis, route)


def statistics(values, frame_mask, length, height):
    clip_count, frames, rows_here, cols, chans = values.shape
    sub = chans // GROUPS
    grouped = values.reshape(clip_count, frames, rows_here, cols, GROUPS, sub)
    mask_six = frame_mask[:, :, :, :, :, None]
    count = (length * (height * cols * sub)).astype(jnp.float32)[:, None]
    total = lax.psum(jnp.sum(grouped * mask_six, axis=(1, 2, 3, 5)), "rows")
    mean = total / count
    centered = grouped - mean[:, None, None, None, :, None]
    spread = lax.psum(jnp.sum(centered * centered * mask_six, axis=(1, 2, 3, 5)), "rows")
    var = spread / count
    rstd = lax.rsqrt(var + eps)
    mean_chan = jnp.repeat(mean, sub, axis=-1)[:, None, None, None, :]
    rstd_chan = jnp.repeat(rstd, sub, axis=-1)[:, None, None, None, :]
    return (mean_chan, rstd_chan)


def block(current, length, weight, gain, shift, bias, height):
    clip_count, frames, rows_here, cols, chans = current.shape
    values = current.astype(jnp.float32)
    frame_mask = (jnp.arange(frames)[None, :] < length[:, None]).astype(jnp.float32)[
        :, :, None, None, None
    ]
    mean_chan, rstd_chan = statistics(values, frame_mask, length, height)
    hidden = jax.nn.silu((values - mean_chan) * rstd_chan * gain + shift).astype(jnp.bfloat16)
    extended = extended_2(hidden, (("rows", 2),), 1)
    padded = jnp.pad(extended, ((0, 0), (0, 0), (0, 0), (1, 1), (0, 0)))
    padded = jnp.concatenate([padded[:, :1], padded[:, :1], padded], axis=1)
    pieces = []
    for tap_t in range(3):
        for tap_h in range(3):
            for tap_w in range(3):
                pieces.append(
                    padded[
                        :,
                        tap_t : tap_t + frames,
                        tap_h : tap_h + rows_here,
                        tap_w : tap_w + cols,
                        :,
                    ]
                )
    patches = jnp.concatenate(pieces, axis=-1).reshape(-1, 27 * chans)
    conv = jnp.dot(patches, weight, preferred_element_type=jnp.float32).reshape(values.shape)
    result = ((values + conv + bias) * frame_mask).astype(jnp.bfloat16)
    return (result, patches, frame_mask.astype(jnp.bfloat16))


def relay(clips, lengths, conv_weight, norm_gain, norm_shift, conv_bias, cotangent):
    segments = lax.axis_size("segment")
    segment_id = lax.axis_index("segment")
    micro = clips.shape[0]
    frames = clips.shape[2]
    cols = clips.shape[4]
    chans = clips.shape[5]
    height = clips.shape[3] * lax.axis_size("rows")
    weight = conv_weight[0]
    gain = norm_gain[0]
    shift = norm_shift[0]
    bias = conv_bias[0]
    cot_all = cotangent[0]
    total_cells = micro * clips.shape[1] * lax.axis_size("dp") * frames * height * cols
    factor = 1.0 / math.sqrt(total_cells)

    def tick(step, carry):
        arrived, stash, grads = carry
        which = step - segment_id
        valid = (which >= 0) & (which < micro)
        slot = jnp.clip(which, 0, micro - 1)
        fresh = lax.dynamic_index_in_dim(
            clips, jnp.clip(step, 0, micro - 1).astype(jnp.int32), 0, keepdims=False
        )
        current = jnp.where(segment_id == 0, fresh, arrived)
        length = lax.dynamic_index_in_dim(lengths, slot, 0, keepdims=False)
        result, patches, mask_five = block(current, length, weight, gain, shift, bias, height)
        cot_now = lax.dynamic_index_in_dim(cot_all, slot, 0, keepdims=False)
        masked = (cot_now * mask_five).reshape(-1, chans)
        term = lax.dot_general(
            patches, masked, (((0,), (0,)), ((), ())), preferred_element_type=jnp.float32
        )
        grads = grads + jnp.where(valid, term, 0.0)
        previous = lax.dynamic_index_in_dim(stash, slot, 0, keepdims=False)
        stash = lax.dynamic_update_index_in_dim(stash, jnp.where(valid, result, previous), slot, 0)
        arrived = passed_along(result, "segment", 1)
        return (arrived, stash, grads)

    start = (
        jnp.zeros(clips.shape[1:], jnp.bfloat16),
        jnp.zeros(clips.shape, jnp.bfloat16),
        jnp.zeros((27 * chans, chans), jnp.float32),
    )
    arrived, stash, grads = lax.fori_loop(0, micro + segments - 1, tick, start)
    grads = lax.psum(grads, ("rows", "dp")) * factor
    return (stash[None], grads[None])


TAPS = 9


def swapped(value, axis, flip):
    return lax.ppermute(value, axis, [(i, i ^ flip) for i in range(lax.axis_size(axis))])


def group_sum(value):
    lane = lax.broadcasted_iota(jnp.int32, value.shape, 1)
    chans = value.shape[1]
    for step in (1, 2):
        after = pltpu.roll(value, chans - step, 1)
        before = pltpu.roll(value, step, 1)
        value = value + jnp.where(lane & step == 0, after, before)
    return value


def normalized(values, length, gain, shift):
    frames = len(values)
    positions, chans = values[0].shape
    mask = [(length > f).astype(jnp.float32) for f in range(frames)]
    count = length * (positions * (chans // GROUPS))

    def masked_sum(arrays):
        parts = [
            jnp.sum(a.reshape(positions // 8, 8, chans), axis=0) * m for a, m in zip(arrays, mask)
        ]
        return group_sum(jnp.sum(sum(parts), axis=0, keepdims=True))

    mean = masked_sum(values) / count
    centered = [v - mean for v in values]
    var = masked_sum([c * c for c in centered]) / count
    rstd = lax.rsqrt(var + eps)
    normed = [c * rstd * gain + shift for c in centered]
    return [v / (1.0 + jnp.exp(-v)) for v in normed]


def taps_of(hidden, cols):
    positions, lanes = hidden.shape
    rows = positions // cols
    zero = jnp.zeros((1, cols, lanes), jnp.float32)
    padded = jnp.concatenate([zero, hidden.reshape(rows, cols, lanes), zero], axis=0)
    col = lax.broadcasted_iota(jnp.int32, padded.shape, 1)
    left = jnp.where(col == 0, 0.0, pltpu.roll(padded, 1, 1))
    right = jnp.where(col == cols - 1, 0.0, pltpu.roll(padded, cols - 1, 1))
    pieces = [
        value[b : b + rows].reshape(positions, lanes).astype(jnp.bfloat16)
        for b in range(3)
        for value in (left, padded, right)
    ]
    return jnp.concatenate(pieces, axis=1)


def convolved(hidden, weight_ref, cols):
    frames = len(hidden)
    chans = hidden[0].shape[1]
    depth = TAPS * chans
    outs = [None] * frames
    for source in range(frames):
        patch = taps_of(hidden[source], cols)
        uses = [(f, a) for f in range(frames) for a in range(3) if max(f + a - 2, 0) == source]
        needed = sorted({a for _, a in uses})
        weight = jnp.concatenate([weight_ref[a * depth : (a + 1) * depth] for a in needed], axis=1)
        product = jnp.dot(patch, weight, preferred_element_type=jnp.float32)
        for f, a in uses:
            at = needed.index(a) * chans
            term = product[:, at : at + chans]
            outs[f] = term if outs[f] is None else outs[f] + term
    return outs


def real_frames(lengths):
    index = lax.broadcasted_iota(jnp.int32, lengths.shape, 1)
    mine = jnp.where(index == lax.axis_index("rows"), lengths[...].astype(jnp.float32), 0.0)
    return jnp.sum(mine, axis=1, keepdims=True)


def split_three(value):
    high = lax.reduce_precision(value, 8, 7)
    rest = value - high
    middle = lax.reduce_precision(rest, 8, 7)
    return jnp.stack([high, middle, rest - middle]).astype(jnp.bfloat16)


def prepare_kernel(lengths, clips, *refs):
    pieces, (arrived, gain, shift, bias, whole, hidden, params) = refs[:3], refs[3:]
    segment, row = lax.axis_index("segment"), lax.axis_index("rows")
    _, frames, span, chans = pieces[0].shape
    for k, piece in enumerate([clips.at[row], *[p.at[0] for p in pieces]]):
        whole[:, pl.ds(pl.multiple_of((row ^ k) * span, span), span), :] = piece[...]
    extra = arrived[arrived.shape[0] - 16 :].astype(jnp.float32)
    sent = [extra[i : i + 1] + extra[i + 3 : i + 4] + extra[i + 6 : i + 7] for i in range(3)]
    own = (gain, shift, bias)
    used = [jnp.where(segment == 0, o[...], s) for o, s in zip(own, sent)]
    values = [whole[f].astype(jnp.float32) for f in range(frames)]
    out = normalized(values, real_frames(lengths), used[0], used[1])
    for f in range(frames):
        hidden[f] = out[f].astype(jnp.bfloat16)
    params[...] = jnp.broadcast_to(used[2], params.shape)


def first_kernel(
    cols, lengths, whole, hidden, own_weight, arrived, other, params, gain, shift, *refs
):
    (mine, near, far, middle, after, weight) = refs
    slices = [mine, near, far.at[0], far.at[1]]
    segment, part = lax.axis_index("segment"), lax.axis_index("dp")
    frames, positions, chans = whole.shape
    real = real_frames(lengths)
    half = own_weight.shape[0] // 2
    core = part & 1

    @pl.when(segment == 0)
    def _():
        weight[...] = own_weight[...]

    @pl.when(segment != 0)
    def _():
        at = pl.multiple_of(core * half, 16)
        weight[pl.ds(at, half)] = arrived[:half]
        at = pl.multiple_of((1 - core) * half, 16)
        weight[pl.ds(at, half)] = other[:half]

    before = [hidden[f].astype(jnp.float32) for f in range(frames)]
    outs = convolved(before, weight, cols)
    bias = params[0:1]
    values = []
    for f in range(frames):
        out = (whole[f].astype(jnp.float32) + outs[f] + bias) * (real > f).astype(jnp.float32)
        middle[f] = out.astype(jnp.bfloat16)
        values.append(middle[f].astype(jnp.float32))
    out = normalized(values, real, gain[...], shift[...])
    out = [o.astype(jnp.bfloat16).astype(jnp.float32) for o in out]
    for f in range(frames):
        after[f] = out[f].astype(jnp.bfloat16)
    chosen = [jnp.where(segment == 0, b, o) for b, o in zip(before, out)]
    quarter = chans // 4
    group = lax.broadcasted_iota(jnp.int32, (positions, chans), 1) // quarter
    for k in range(4):
        packed = None
        for f in range(frames):
            moved = pltpu.roll(chosen[f], ((f - (part ^ k)) & 3) * quarter, 1)
            packed = moved if packed is None else jnp.where(group == f, moved, packed)
        slices[k][...] = packed.astype(jnp.bfloat16)


def second_kernel(cols, lengths, middle, after, weight, bias, *refs):
    mine, outer, inner, stash = refs
    pieces = [mine, outer.at[0], inner, outer.at[1]]
    segment, row = lax.axis_index("segment"), lax.axis_index("rows")
    frames, positions, chans = middle.shape
    span = positions // 4
    real = real_frames(lengths)

    @pl.when(segment == 0)
    def _():
        stash[...] = middle[...]

    @pl.when(segment != 0)
    def _():
        outs = convolved([after[f].astype(jnp.float32) for f in range(frames)], weight, cols)
        for f in range(frames):
            out = middle[f].astype(jnp.float32) + outs[f] + bias[...]
            stash[f] = (out * (real > f).astype(jnp.float32)).astype(jnp.bfloat16)

    for k, piece in enumerate(pieces):
        piece[...] = stash[:, pl.ds(pl.multiple_of((row ^ k) * span, span), span), :]


def cotangent_kernel(early, late, turned, whole):
    row = lax.axis_index("rows")
    _, frames, span, chans = early.shape
    for k, piece in enumerate([early.at[0], early.at[1], late.at[0], late.at[1]]):
        whole[:, pl.ds(pl.multiple_of((row ^ k) * span, span), span), :] = piece[...]
    for f in range(frames):
        turned[f * chans : (f + 1) * chans] = whole[f].astype(jnp.float32).T.astype(jnp.bfloat16)


def gradient_kernel(cols, *refs):
    slices, cots, (send, keep, grad) = refs[:4], refs[4:8], refs[8:]
    row = lax.axis_index("rows")
    chans = slices[0].shape[1]
    quarter = chans // 4
    patches = jnp.concatenate([taps_of(s[...].astype(jnp.float32), cols) for s in slices], axis=0)
    left = jnp.concatenate([c[...] for c in cots], axis=1)
    product = jnp.dot(left, patches, preferred_element_type=jnp.float32)
    group = lax.broadcasted_iota(jnp.int32, (chans, chans), 1) // quarter
    for tap in range(TAPS):
        total = None
        for f in range(4):
            value = product[f * chans : (f + 1) * chans, tap * chans : (tap + 1) * chans]
            moved = None
            for a in range(3):
                by = (a - max(f + a - 2, 0)) * quarter % chans
                turned = pltpu.roll(value, by, 1) if by else value
                moved = turned if moved is None else jnp.where(group == a, turned, moved)
            total = moved if total is None else total + moved
        total = total.T
        for a in range(3):
            grad[a * TAPS + tap] = total[a * quarter : (a + 1) * quarter]
    low = row & 1
    part = quarter // 2
    there = grad[:, pl.ds(pl.multiple_of((1 - low) * part, part), part), :]
    send[...] = there.reshape(send.shape).astype(jnp.bfloat16)
    keep[...] = grad[:, pl.ds(pl.multiple_of(low * part, part), part), :].reshape(keep.shape)


def finish_kernel(total, lower, across, last, beside, last_beside, *refs):
    pieces, (grads, stash) = refs[:4], refs[4:]
    row, part = lax.axis_index("rows"), lax.axis_index("dp")
    taps = grads.shape[0]
    sources = (total, lower, across, last)
    sources += (beside.at[0], beside.at[1], beside.at[2], last_beside)
    for n, source in enumerate(sources):
        i, j, k = n >> 2, n >> 1 & 1, n & 1
        at = (part ^ (i + 2 * j)) * 32 + ((row & 1) ^ k) * 16
        value = source[...].astype(jnp.float32).reshape(taps, 16, grads.shape[2])
        grads[:, pl.ds(pl.multiple_of(at, 16), 16), :] = value
    for k, piece in enumerate(pieces):
        stash[pl.ds(row ^ k, 1)] = piece[...][None]


def whole_clips(clips, lengths, conv_weight, norm_gain, norm_shift, conv_bias, cotangent):
    row = lax.axis_index("rows")
    part = lax.axis_index("dp")
    micro, _, frames, rows_here, cols, chans = clips.shape
    span = rows_here * cols
    positions = span * micro
    total_cells = micro * lax.axis_size("dp") * frames * positions
    factor = 1.0 / math.sqrt(total_cells)
    core = part & 1
    weight = conv_weight[0]
    half = weight.shape[0] // 2
    bf16, f32 = jnp.bfloat16, jnp.float32
    shape = jax.ShapeDtypeStruct
    vmem = pl.BlockSpec(memory_space=pltpu.VMEM)
    params = pltpu.CompilerParams(vmem_limit_bytes=48 * 1024 * 1024)

    def call(kernel, outs, scratch, args):
        return pl.pallas_call(
            kernel,
            out_shape=outs,
            in_specs=[vmem] * len(args),
            out_specs=[vmem] * len(outs),
            scratch_shapes=scratch,
            compiler_params=params,
        )(*args)

    clip_like = shape((frames, positions, chans), bf16)
    piece_like = shape((frames, span, chans), bf16)

    clips_here = clips.reshape(micro, frames, span, chans)
    cot_here = cotangent.reshape(micro, frames, span, chans)
    lengths = jnp.transpose(lengths)

    extras = split_three(jnp.concatenate([norm_gain, norm_shift, conv_bias])).reshape(9, chans)
    extras = jnp.pad(extras, ((0, 7), (0, 0)))
    mine = lax.dynamic_slice_in_dim(weight, core * half, half)
    arrived = lax.ppermute(jnp.concatenate([mine, extras]), "segment", [(0, 1)])

    def spread(pieces):
        return [swapped(piece, "rows", k + 1) for k, piece in enumerate(pieces)]

    pieces = []
    for k in range(1, micro):
        both = [lax.dynamic_index_in_dim(v, row ^ k, 0) for v in (clips_here, cot_here)]
        pieces.append(jnp.concatenate(both))
    pieces = spread(pieces)

    length = lax.dynamic_index_in_dim(lengths[0], row, 0, keepdims=False)
    mask = (jnp.arange(frames) < length).astype(bf16)[:, None, None]
    own_cot = lax.dynamic_index_in_dim(cot_here, row, 0, keepdims=False)
    early = jnp.stack([own_cot, pieces[0][1]]) * mask
    early_across = swapped(early, "dp", 2)
    pieces[1:], early_across = lax.optimization_barrier((pieces[1:], early_across))
    late = jnp.stack([pieces[1][1], pieces[2][1]]) * mask
    pieces, late, arrived = lax.optimization_barrier((pieces, late, arrived))
    late_across = swapped(late, "dp", 2)

    def turned(first, second):
        return call(
            cotangent_kernel,
            [shape((frames * chans, positions), bf16)],
            [pltpu.VMEM((frames, positions, chans), bf16)],
            [first, second],
        )[0]

    cots = {0: turned(early, late)}
    cots[1] = swapped(cots[0], "dp", 1)

    other = swapped(arrived, "dp", 1)
    whole, hidden, bias0 = call(
        prepare_kernel,
        [clip_like, clip_like, shape((8, chans), f32)],
        [],
        [lengths, clips_here, *pieces, arrived, norm_gain, norm_shift, conv_bias],
    )

    slice_like = shape((positions, chans), bf16)
    mine, near, far, middle, after = call(
        functools.partial(first_kernel, cols),
        [slice_like, slice_like, shape((2, positions, chans), bf16), clip_like, clip_like],
        [pltpu.VMEM(weight.shape, bf16)],
        [lengths, whole, hidden, weight, arrived, other, bias0, norm_gain, norm_shift],
    )
    far = swapped(far, "dp", 2)

    own_piece, outer, inner = call(
        functools.partial(second_kernel, cols),
        [piece_like, shape((2, *piece_like.shape), bf16), piece_like],
        [pltpu.VMEM((frames, positions, chans), bf16)],
        [lengths, middle, after, weight, conv_bias],
    )
    far, late_across, outer, cots[1] = lax.optimization_barrier(
        (far, late_across, outer, cots[1])
    )
    cots[2] = turned(early_across, late_across)
    cots[3] = swapped(cots[2], "dp", 1)
    near = swapped(jnp.stack([near, far[1]]), "dp", 1)
    outer = swapped(outer, "rows", 1)
    held = [mine, near[0], far[0], near[1]]

    quarter = chans // 4
    rows_sent = 27 * quarter // 2
    send, keep = call(
        functools.partial(gradient_kernel, cols),
        [shape((rows_sent, chans), bf16), shape((rows_sent, chans), f32)],
        [pltpu.VMEM((27, quarter, chans), f32)],
        [*held, *[cots[k] for k in range(4)]],
    )
    send, outer = lax.optimization_barrier((send, outer))
    got = swapped(send, "rows", 1)
    total = (keep + got.astype(f32)).astype(bf16)
    total = (total.astype(f32) + swapped(total, "rows", 2).astype(f32)) * factor
    total = total.astype(bf16)
    total, inner, outer = lax.optimization_barrier((total, inner, outer))
    inner = swapped(jnp.stack([inner, outer[1]]), "rows", 2)
    lower = swapped(total, "rows", 1)
    across = swapped(total, "dp", 2)
    last, inner = lax.optimization_barrier((swapped(lower, "dp", 2), inner))
    beside = swapped(jnp.stack([total, lower, across]), "dp", 1)
    grads, stash = call(
        finish_kernel,
        [shape((27, chans, chans), f32), shape((micro, frames, span, chans), bf16)],
        [],
        [
            *[total, lower, across, last, beside, swapped(last, "dp", 1)],
            *[own_piece, outer[0], inner[0], inner[1]],
        ],
    )
    return (stash.reshape((1,) + clips.shape), grads.reshape(1, 27 * chans, chans))


def per_device(clips, lengths, conv_weight, norm_gain, norm_shift, conv_bias, cotangent):
    sizes = [lax.axis_size(axis) for axis in ("segment", "rows", "dp")]
    fits = sizes == [2, 4, 4] and clips.shape[0] == 4 and clips.shape[1] == 1
    plan = whole_clips if fits and clips.shape[5] == 128 else relay
    return plan(clips, lengths, conv_weight, norm_gain, norm_shift, conv_bias, cotangent)


def solution(mesh):
    in_specs = (
        P(None, "dp", None, "rows", None, None),
        P(None, "dp"),
        P("segment", None, None),
        P("segment", None),
        P("segment", None),
        P("segment", None),
        P("segment", None, "dp", None, "rows", None, None),
    )
    out_specs = (P("segment", None, "dp", None, "rows", None, None), P("segment", None, None))
    return jax.shard_map(
        per_device, mesh=mesh, in_specs=in_specs, out_specs=out_specs, check_vma=False
    )
```

```python
import functools
import math

import jax
import jax.numpy as jnp
from jax import lax
from jax.experimental import pallas as pl
from jax.experimental.pallas import tpu as pltpu
from jax.sharding import PartitionSpec as P

GROUPS = 32


eps = 1e-06


def extended_2(cells, sides, width):
    for axis, dim in sides:
        count = lax.axis_size(axis)
        ends = count - 1
        head = lax.slice_in_dim(cells, 0, width, axis=dim)
        tail = lax.slice_in_dim(cells, cells.shape[dim] - width, cells.shape[dim], axis=dim)
        cells = jnp.concatenate(
            [
                lax.ppermute(tail, axis, [(i, (i + 1) % count) for i in range(ends)]),
                cells,
                lax.ppermute(head, axis, [((i + 1) % count, i) for i in range(ends)]),
            ],
            axis=dim,
        )
    return cells


def passed_along(block, axis, distance):
    devices = range(lax.axis_size(axis))
    route = [(i - distance, i) for i in devices if i - distance in devices]
    return lax.ppermute(block, axis, route)


def statistics(values, frame_mask, length, height):
    clip_count, frames, rows_here, cols, chans = values.shape
    sub = chans // GROUPS
    grouped = values.reshape(clip_count, frames, rows_here, cols, GROUPS, sub)
    mask_six = frame_mask[:, :, :, :, :, None]
    count = (length * (height * cols * sub)).astype(jnp.float32)[:, None]
    total = lax.psum(jnp.sum(grouped * mask_six, axis=(1, 2, 3, 5)), "rows")
    mean = total / count
    centered = grouped - mean[:, None, None, None, :, None]
    spread = lax.psum(jnp.sum(centered * centered * mask_six, axis=(1, 2, 3, 5)), "rows")
    var = spread / count
    rstd = lax.rsqrt(var + eps)
    mean_chan = jnp.repeat(mean, sub, axis=-1)[:, None, None, None, :]
    rstd_chan = jnp.repeat(rstd, sub, axis=-1)[:, None, None, None, :]
    return (mean_chan, rstd_chan)


def block(current, length, weight, gain, shift, bias, height):
    clip_count, frames, rows_here, cols, chans = current.shape
    values = current.astype(jnp.float32)
    frame_mask = (jnp.arange(frames)[None, :] < length[:, None]).astype(jnp.float32)[
        :, :, None, None, None
    ]
    mean_chan, rstd_chan = statistics(values, frame_mask, length, height)
    hidden = jax.nn.silu((values - mean_chan) * rstd_chan * gain + shift).astype(jnp.bfloat16)
    extended = extended_2(hidden, (("rows", 2),), 1)
    padded = jnp.pad(extended, ((0, 0), (0, 0), (0, 0), (1, 1), (0, 0)))
    padded = jnp.concatenate([padded[:, :1], padded[:, :1], padded], axis=1)
    pieces = []
    for tap_t in range(3):
        for tap_h in range(3):
            for tap_w in range(3):
                pieces.append(
                    padded[
                        :,
                        tap_t : tap_t + frames,
                        tap_h : tap_h + rows_here,
                        tap_w : tap_w + cols,
                        :,
                    ]
                )
    patches = jnp.concatenate(pieces, axis=-1).reshape(-1, 27 * chans)
    conv = jnp.dot(patches, weight, preferred_element_type=jnp.float32).reshape(values.shape)
    result = ((values + conv + bias) * frame_mask).astype(jnp.bfloat16)
    return (result, patches, frame_mask.astype(jnp.bfloat16))


def relay(clips, lengths, conv_weight, norm_gain, norm_shift, conv_bias, cotangent):
    segments = lax.axis_size("segment")
    segment_id = lax.axis_index("segment")
    micro = clips.shape[0]
    frames = clips.shape[2]
    cols = clips.shape[4]
    chans = clips.shape[5]
    height = clips.shape[3] * lax.axis_size("rows")
    weight = conv_weight[0]
    gain = norm_gain[0]
    shift = norm_shift[0]
    bias = conv_bias[0]
    cot_all = cotangent[0]
    total_cells = micro * clips.shape[1] * lax.axis_size("dp") * frames * height * cols
    factor = 1.0 / math.sqrt(total_cells)

    def tick(step, carry):
        arrived, stash, grads = carry
        which = step - segment_id
        valid = (which >= 0) & (which < micro)
        slot = jnp.clip(which, 0, micro - 1)
        fresh = lax.dynamic_index_in_dim(
            clips, jnp.clip(step, 0, micro - 1).astype(jnp.int32), 0, keepdims=False
        )
        current = jnp.where(segment_id == 0, fresh, arrived)
        length = lax.dynamic_index_in_dim(lengths, slot, 0, keepdims=False)
        result, patches, mask_five = block(current, length, weight, gain, shift, bias, height)
        cot_now = lax.dynamic_index_in_dim(cot_all, slot, 0, keepdims=False)
        masked = (cot_now * mask_five).reshape(-1, chans)
        term = lax.dot_general(
            patches, masked, (((0,), (0,)), ((), ())), preferred_element_type=jnp.float32
        )
        grads = grads + jnp.where(valid, term, 0.0)
        previous = lax.dynamic_index_in_dim(stash, slot, 0, keepdims=False)
        stash = lax.dynamic_update_index_in_dim(stash, jnp.where(valid, result, previous), slot, 0)
        arrived = passed_along(result, "segment", 1)
        return (arrived, stash, grads)

    start = (
        jnp.zeros(clips.shape[1:], jnp.bfloat16),
        jnp.zeros(clips.shape, jnp.bfloat16),
        jnp.zeros((27 * chans, chans), jnp.float32),
    )
    arrived, stash, grads = lax.fori_loop(0, micro + segments - 1, tick, start)
    grads = lax.psum(grads, ("rows", "dp")) * factor
    return (stash[None], grads[None])


TAPS = 9


def swapped(value, axis, flip):
    return lax.ppermute(value, axis, [(i, i ^ flip) for i in range(lax.axis_size(axis))])


def group_sum(value):
    lane = lax.broadcasted_iota(jnp.int32, value.shape, 1)
    chans = value.shape[1]
    for step in (1, 2):
        after = pltpu.roll(value, chans - step, 1)
        before = pltpu.roll(value, step, 1)
        value = value + jnp.where(lane & step == 0, after, before)
    return value


def normalized(values, length, gain, shift):
    frames = len(values)
    positions, chans = values[0].shape
    mask = [(length > f).astype(jnp.float32) for f in range(frames)]
    count = length * (positions * (chans // GROUPS))

    def masked_sum(arrays):
        parts = [
            jnp.sum(a.reshape(positions // 8, 8, chans), axis=0) * m for a, m in zip(arrays, mask)
        ]
        return group_sum(jnp.sum(sum(parts), axis=0, keepdims=True))

    mean = masked_sum(values) / count
    centered = [v - mean for v in values]
    var = masked_sum([c * c for c in centered]) / count
    rstd = lax.rsqrt(var + eps)
    normed = [c * rstd * gain + shift for c in centered]
    return [v / (1.0 + jnp.exp(-v)) for v in normed]


def taps_of(hidden, cols):
    positions, lanes = hidden.shape
    rows = positions // cols
    zero = jnp.zeros((1, cols, lanes), jnp.float32)
    padded = jnp.concatenate([zero, hidden.reshape(rows, cols, lanes), zero], axis=0)
    col = lax.broadcasted_iota(jnp.int32, padded.shape, 1)
    left = jnp.where(col == 0, 0.0, pltpu.roll(padded, 1, 1))
    right = jnp.where(col == cols - 1, 0.0, pltpu.roll(padded, cols - 1, 1))
    pieces = [
        value[b : b + rows].reshape(positions, lanes).astype(jnp.bfloat16)
        for b in range(3)
        for value in (left, padded, right)
    ]
    return jnp.concatenate(pieces, axis=1)


def convolved(hidden, weight_ref, cols):
    frames = len(hidden)
    chans = hidden[0].shape[1]
    depth = TAPS * chans
    outs = [None] * frames
    for source in range(frames):
        patch = taps_of(hidden[source], cols)
        uses = [(f, a) for f in range(frames) for a in range(3) if max(f + a - 2, 0) == source]
        needed = sorted({a for _, a in uses})
        weight = jnp.concatenate([weight_ref[a * depth : (a + 1) * depth] for a in needed], axis=1)
        product = jnp.dot(patch, weight, preferred_element_type=jnp.float32)
        for f, a in uses:
            at = needed.index(a) * chans
            term = product[:, at : at + chans]
            outs[f] = term if outs[f] is None else outs[f] + term
    return outs


def real_frames(lengths):
    index = lax.broadcasted_iota(jnp.int32, lengths.shape, 1)
    mine = jnp.where(index == lax.axis_index("rows"), lengths[...].astype(jnp.float32), 0.0)
    return jnp.sum(mine, axis=1, keepdims=True)


def split_three(value):
    high = lax.reduce_precision(value, 8, 7)
    rest = value - high
    middle = lax.reduce_precision(rest, 8, 7)
    return jnp.stack([high, middle, rest - middle]).astype(jnp.bfloat16)


def prepare_kernel(lengths, clips, *refs):
    pieces, (arrived, gain, shift, bias, whole, hidden, params) = refs[:3], refs[3:]
    segment, row = lax.axis_index("segment"), lax.axis_index("rows")
    _, frames, span, chans = pieces[0].shape
    for k, piece in enumerate([clips.at[row], *[p.at[0] for p in pieces]]):
        whole[:, pl.ds(pl.multiple_of((row ^ k) * span, span), span), :] = piece[...]
    extra = arrived[arrived.shape[0] - 16 :].astype(jnp.float32)
    sent = [extra[i : i + 1] + extra[i + 3 : i + 4] + extra[i + 6 : i + 7] for i in range(3)]
    own = (gain, shift, bias)
    used = [jnp.where(segment == 0, o[...], s) for o, s in zip(own, sent)]
    values = [whole[f].astype(jnp.float32) for f in range(frames)]
    out = normalized(values, real_frames(lengths), used[0], used[1])
    for f in range(frames):
        hidden[f] = out[f].astype(jnp.bfloat16)
    params[...] = jnp.broadcast_to(used[2], params.shape)


def first_kernel(
    cols, lengths, whole, hidden, own_weight, arrived, other, params, gain, shift, *refs
):
    (mine, near, far, middle, after, weight) = refs
    slices = [mine, near, far.at[0], far.at[1]]
    segment, part = lax.axis_index("segment"), lax.axis_index("dp")
    frames, positions, chans = whole.shape
    real = real_frames(lengths)
    half = own_weight.shape[0] // 2
    core = part & 1

    @pl.when(segment == 0)
    def _():
        weight[...] = own_weight[...]

    @pl.when(segment != 0)
    def _():
        at = pl.multiple_of(core * half, 16)
        weight[pl.ds(at, half)] = arrived[:half]
        at = pl.multiple_of((1 - core) * half, 16)
        weight[pl.ds(at, half)] = other[:half]

    before = [hidden[f].astype(jnp.float32) for f in range(frames)]
    outs = convolved(before, weight, cols)
    bias = params[0:1]
    values = []
    for f in range(frames):
        out = (whole[f].astype(jnp.float32) + outs[f] + bias) * (real > f).astype(jnp.float32)
        middle[f] = out.astype(jnp.bfloat16)
        values.append(middle[f].astype(jnp.float32))
    out = normalized(values, real, gain[...], shift[...])
    out = [o.astype(jnp.bfloat16).astype(jnp.float32) for o in out]
    for f in range(frames):
        after[f] = out[f].astype(jnp.bfloat16)
    chosen = [jnp.where(segment == 0, b, o) for b, o in zip(before, out)]
    quarter = chans // 4
    group = lax.broadcasted_iota(jnp.int32, (positions, chans), 1) // quarter
    for k in range(4):
        packed = None
        for f in range(frames):
            moved = pltpu.roll(chosen[f], ((f - (part ^ k)) & 3) * quarter, 1)
            packed = moved if packed is None else jnp.where(group == f, moved, packed)
        slices[k][...] = packed.astype(jnp.bfloat16)


def second_kernel(cols, lengths, middle, after, weight, bias, *refs):
    mine, outer, inner, stash = refs
    pieces = [mine, outer.at[0], inner, outer.at[1]]
    segment, row = lax.axis_index("segment"), lax.axis_index("rows")
    frames, positions, chans = middle.shape
    span = positions // 4
    real = real_frames(lengths)

    @pl.when(segment == 0)
    def _():
        stash[...] = middle[...]

    @pl.when(segment != 0)
    def _():
        outs = convolved([after[f].astype(jnp.float32) for f in range(frames)], weight, cols)
        for f in range(frames):
            out = middle[f].astype(jnp.float32) + outs[f] + bias[...]
            stash[f] = (out * (real > f).astype(jnp.float32)).astype(jnp.bfloat16)

    for k, piece in enumerate(pieces):
        piece[...] = stash[:, pl.ds(pl.multiple_of((row ^ k) * span, span), span), :]


def cotangent_kernel(early, late, turned, whole):
    row = lax.axis_index("rows")
    _, frames, span, chans = early.shape
    for k, piece in enumerate([early.at[0], early.at[1], late.at[0], late.at[1]]):
        whole[:, pl.ds(pl.multiple_of((row ^ k) * span, span), span), :] = piece[...]
    for f in range(frames):
        turned[f * chans : (f + 1) * chans] = whole[f].astype(jnp.float32).T.astype(jnp.bfloat16)


def gradient_kernel(cols, *refs):
    slices, cots, (send, keep, grad) = refs[:4], refs[4:8], refs[8:]
    row = lax.axis_index("rows")
    chans = slices[0].shape[1]
    quarter = chans // 4
    patches = jnp.concatenate([taps_of(s[...].astype(jnp.float32), cols) for s in slices], axis=0)
    left = jnp.concatenate([c[...] for c in cots], axis=1)
    product = jnp.dot(left, patches, preferred_element_type=jnp.float32)
    group = lax.broadcasted_iota(jnp.int32, (chans, chans), 1) // quarter
    for tap in range(TAPS):
        total = None
        for f in range(4):
            value = product[f * chans : (f + 1) * chans, tap * chans : (tap + 1) * chans]
            moved = None
            for a in range(3):
                by = (a - max(f + a - 2, 0)) * quarter % chans
                turned = pltpu.roll(value, by, 1) if by else value
                moved = turned if moved is None else jnp.where(group == a, turned, moved)
            total = moved if total is None else total + moved
        total = total.T
        for a in range(3):
            grad[a * TAPS + tap] = total[a * quarter : (a + 1) * quarter]
    low = row & 1
    part = quarter // 2
    there = grad[:, pl.ds(pl.multiple_of((1 - low) * part, part), part), :]
    send[...] = there.reshape(send.shape).astype(jnp.bfloat16)
    keep[...] = grad[:, pl.ds(pl.multiple_of(low * part, part), part), :].reshape(keep.shape)


def finish_kernel(total, lower, across, last, beside, opposite, *refs):
    pieces, (grads, stash) = refs[:4], refs[4:]
    row, part = lax.axis_index("rows"), lax.axis_index("dp")
    taps = grads.shape[0]
    sources = (total, lower, across, last)
    sources += (beside.at[0], beside.at[1], opposite.at[0], opposite.at[1])
    for n, source in enumerate(sources):
        i, j, k = n >> 2, n >> 1 & 1, n & 1
        at = (part ^ (i + 2 * j)) * 32 + ((row & 1) ^ k) * 16
        value = source[...].astype(jnp.float32).reshape(taps, 16, grads.shape[2])
        grads[:, pl.ds(pl.multiple_of(at, 16), 16), :] = value
    for k, piece in enumerate(pieces):
        stash[pl.ds(row ^ k, 1)] = piece[...][None]


def whole_clips(clips, lengths, conv_weight, norm_gain, norm_shift, conv_bias, cotangent):
    row = lax.axis_index("rows")
    part = lax.axis_index("dp")
    micro, _, frames, rows_here, cols, chans = clips.shape
    span = rows_here * cols
    positions = span * micro
    total_cells = micro * lax.axis_size("dp") * frames * positions
    factor = 1.0 / math.sqrt(total_cells)
    core = part & 1
    weight = conv_weight[0]
    half = weight.shape[0] // 2
    bf16, f32 = jnp.bfloat16, jnp.float32
    shape = jax.ShapeDtypeStruct
    vmem = pl.BlockSpec(memory_space=pltpu.VMEM)
    params = pltpu.CompilerParams(vmem_limit_bytes=48 * 1024 * 1024)

    def call(kernel, outs, scratch, args):
        return pl.pallas_call(
            kernel,
            out_shape=outs,
            in_specs=[vmem] * len(args),
            out_specs=[vmem] * len(outs),
            scratch_shapes=scratch,
            compiler_params=params,
        )(*args)

    clip_like = shape((frames, positions, chans), bf16)
    piece_like = shape((frames, span, chans), bf16)

    clips_here = clips.reshape(micro, frames, span, chans)
    cot_here = cotangent.reshape(micro, frames, span, chans)
    lengths = jnp.transpose(lengths)

    extras = split_three(jnp.concatenate([norm_gain, norm_shift, conv_bias])).reshape(9, chans)
    extras = jnp.pad(extras, ((0, 7), (0, 0)))
    mine = lax.dynamic_slice_in_dim(weight, core * half, half)
    arrived = lax.ppermute(jnp.concatenate([mine, extras]), "segment", [(0, 1)])

    def both(k):
        sent = [lax.dynamic_index_in_dim(v, row ^ k, 0) for v in (clips_here, cot_here)]
        return swapped(jnp.concatenate(sent), "rows", k)

    pieces = [both(k) for k in (1, 2, 3)]

    length = lax.dynamic_index_in_dim(lengths[0], row, 0, keepdims=False)
    mask = (jnp.arange(frames) < length).astype(bf16)[:, None, None]
    own_cot = lax.dynamic_index_in_dim(cot_here, row, 0, keepdims=False)
    early = jnp.stack([own_cot, pieces[0][1]]) * mask
    early_across = swapped(early, "dp", 2)
    pieces[1:], early_across = lax.optimization_barrier((pieces[1:], early_across))
    late = jnp.stack([pieces[1][1], pieces[2][1]]) * mask
    pieces, late, arrived = lax.optimization_barrier((pieces, late, arrived))
    late_across = swapped(late, "dp", 2)

    def turned(first, second):
        return call(
            cotangent_kernel,
            [shape((frames * chans, positions), bf16)],
            [pltpu.VMEM((frames, positions, chans), bf16)],
            [first, second],
        )[0]

    cots = {0: turned(early, late)}
    cots[1] = swapped(cots[0], "dp", 1)

    other = swapped(arrived, "dp", 1)
    whole, hidden, bias0 = call(
        prepare_kernel,
        [clip_like, clip_like, shape((8, chans), f32)],
        [],
        [lengths, clips_here, *pieces, arrived, norm_gain, norm_shift, conv_bias],
    )

    slice_like = shape((positions, chans), bf16)
    mine, near, far, middle, after = call(
        functools.partial(first_kernel, cols),
        [slice_like, slice_like, shape((2, positions, chans), bf16), clip_like, clip_like],
        [pltpu.VMEM(weight.shape, bf16)],
        [lengths, whole, hidden, weight, arrived, other, bias0, norm_gain, norm_shift],
    )
    far = swapped(far, "dp", 2)

    own_piece, outer, inner = call(
        functools.partial(second_kernel, cols),
        [piece_like, shape((2, *piece_like.shape), bf16), piece_like],
        [pltpu.VMEM((frames, positions, chans), bf16)],
        [lengths, middle, after, weight, conv_bias],
    )
    far, late_across, outer, cots[1] = lax.optimization_barrier(
        (far, late_across, outer, cots[1])
    )
    cots[2] = turned(early_across, late_across)
    cots[3] = swapped(cots[2], "dp", 1)
    near = swapped(jnp.stack([near, far[1]]), "dp", 1)
    outer = swapped(outer, "rows", 1)
    held = [mine, near[0], far[0], near[1]]

    quarter = chans // 4
    rows_sent = 27 * quarter // 2
    send, keep = call(
        functools.partial(gradient_kernel, cols),
        [shape((rows_sent, chans), bf16), shape((rows_sent, chans), f32)],
        [pltpu.VMEM((27, quarter, chans), f32)],
        [*held, *[cots[k] for k in range(4)]],
    )
    send, outer = lax.optimization_barrier((send, outer))
    got = swapped(send, "rows", 1)
    total = (keep + got.astype(f32)).astype(bf16)
    total = (total.astype(f32) + swapped(total, "rows", 2).astype(f32)) * factor
    total = total.astype(bf16)
    total, inner, outer = lax.optimization_barrier((total, inner, outer))
    inner = swapped(jnp.stack([inner, outer[1]]), "rows", 2)
    lower = swapped(total, "rows", 1)
    across = swapped(total, "dp", 2)
    last, inner, across = lax.optimization_barrier((swapped(lower, "dp", 2), inner, across))
    beside = swapped(jnp.stack([total, lower]), "dp", 1)
    opposite = swapped(jnp.stack([across, last]), "dp", 1)
    grads, stash = call(
        finish_kernel,
        [shape((27, chans, chans), f32), shape((micro, frames, span, chans), bf16)],
        [],
        [
            *[total, lower, across, last, beside, opposite],
            *[own_piece, outer[0], inner[0], inner[1]],
        ],
    )
    return (stash.reshape((1,) + clips.shape), grads.reshape(1, 27 * chans, chans))


def per_device(clips, lengths, conv_weight, norm_gain, norm_shift, conv_bias, cotangent):
    sizes = [lax.axis_size(axis) for axis in ("segment", "rows", "dp")]
    fits = sizes == [2, 4, 4] and clips.shape[0] == 4 and clips.shape[1] == 1
    plan = whole_clips if fits and clips.shape[5] == 128 else relay
    return plan(clips, lengths, conv_weight, norm_gain, norm_shift, conv_bias, cotangent)


def solution(mesh):
    in_specs = (
        P(None, "dp", None, "rows", None, None),
        P(None, "dp"),
        P("segment", None, None),
        P("segment", None),
        P("segment", None),
        P("segment", None),
        P("segment", None, "dp", None, "rows", None, None),
    )
    out_specs = (P("segment", None, "dp", None, "rows", None, None), P("segment", None, None))
    return jax.shard_map(
        per_device, mesh=mesh, in_specs=in_specs, out_specs=out_specs, check_vma=False
    )
```

```python
import functools
import math

import jax
import jax.numpy as jnp
from jax import lax
from jax.experimental import pallas as pl
from jax.experimental.pallas import tpu as pltpu
from jax.sharding import PartitionSpec as P

GROUPS = 32


eps = 1e-06


def extended_2(cells, sides, width):
    for axis, dim in sides:
        count = lax.axis_size(axis)
        ends = count - 1
        head = lax.slice_in_dim(cells, 0, width, axis=dim)
        tail = lax.slice_in_dim(cells, cells.shape[dim] - width, cells.shape[dim], axis=dim)
        cells = jnp.concatenate(
            [
                lax.ppermute(tail, axis, [(i, (i + 1) % count) for i in range(ends)]),
                cells,
                lax.ppermute(head, axis, [((i + 1) % count, i) for i in range(ends)]),
            ],
            axis=dim,
        )
    return cells


def passed_along(block, axis, distance):
    devices = range(lax.axis_size(axis))
    route = [(i - distance, i) for i in devices if i - distance in devices]
    return lax.ppermute(block, axis, route)


def statistics(values, frame_mask, length, height):
    clip_count, frames, rows_here, cols, chans = values.shape
    sub = chans // GROUPS
    grouped = values.reshape(clip_count, frames, rows_here, cols, GROUPS, sub)
    mask_six = frame_mask[:, :, :, :, :, None]
    count = (length * (height * cols * sub)).astype(jnp.float32)[:, None]
    total = lax.psum(jnp.sum(grouped * mask_six, axis=(1, 2, 3, 5)), "rows")
    mean = total / count
    centered = grouped - mean[:, None, None, None, :, None]
    spread = lax.psum(jnp.sum(centered * centered * mask_six, axis=(1, 2, 3, 5)), "rows")
    var = spread / count
    rstd = lax.rsqrt(var + eps)
    mean_chan = jnp.repeat(mean, sub, axis=-1)[:, None, None, None, :]
    rstd_chan = jnp.repeat(rstd, sub, axis=-1)[:, None, None, None, :]
    return (mean_chan, rstd_chan)


def block(current, length, weight, gain, shift, bias, height):
    clip_count, frames, rows_here, cols, chans = current.shape
    values = current.astype(jnp.float32)
    frame_mask = (jnp.arange(frames)[None, :] < length[:, None]).astype(jnp.float32)[
        :, :, None, None, None
    ]
    mean_chan, rstd_chan = statistics(values, frame_mask, length, height)
    hidden = jax.nn.silu((values - mean_chan) * rstd_chan * gain + shift).astype(jnp.bfloat16)
    extended = extended_2(hidden, (("rows", 2),), 1)
    padded = jnp.pad(extended, ((0, 0), (0, 0), (0, 0), (1, 1), (0, 0)))
    padded = jnp.concatenate([padded[:, :1], padded[:, :1], padded], axis=1)
    pieces = []
    for tap_t in range(3):
        for tap_h in range(3):
            for tap_w in range(3):
                pieces.append(
                    padded[
                        :,
                        tap_t : tap_t + frames,
                        tap_h : tap_h + rows_here,
                        tap_w : tap_w + cols,
                        :,
                    ]
                )
    patches = jnp.concatenate(pieces, axis=-1).reshape(-1, 27 * chans)
    conv = jnp.dot(patches, weight, preferred_element_type=jnp.float32).reshape(values.shape)
    result = ((values + conv + bias) * frame_mask).astype(jnp.bfloat16)
    return (result, patches, frame_mask.astype(jnp.bfloat16))


def relay(clips, lengths, conv_weight, norm_gain, norm_shift, conv_bias, cotangent):
    segments = lax.axis_size("segment")
    segment_id = lax.axis_index("segment")
    micro = clips.shape[0]
    frames = clips.shape[2]
    cols = clips.shape[4]
    chans = clips.shape[5]
    height = clips.shape[3] * lax.axis_size("rows")
    weight = conv_weight[0]
    gain = norm_gain[0]
    shift = norm_shift[0]
    bias = conv_bias[0]
    cot_all = cotangent[0]
    total_cells = micro * clips.shape[1] * lax.axis_size("dp") * frames * height * cols
    factor = 1.0 / math.sqrt(total_cells)

    def tick(step, carry):
        arrived, stash, grads = carry
        which = step - segment_id
        valid = (which >= 0) & (which < micro)
        slot = jnp.clip(which, 0, micro - 1)
        fresh = lax.dynamic_index_in_dim(
            clips, jnp.clip(step, 0, micro - 1).astype(jnp.int32), 0, keepdims=False
        )
        current = jnp.where(segment_id == 0, fresh, arrived)
        length = lax.dynamic_index_in_dim(lengths, slot, 0, keepdims=False)
        result, patches, mask_five = block(current, length, weight, gain, shift, bias, height)
        cot_now = lax.dynamic_index_in_dim(cot_all, slot, 0, keepdims=False)
        masked = (cot_now * mask_five).reshape(-1, chans)
        term = lax.dot_general(
            patches, masked, (((0,), (0,)), ((), ())), preferred_element_type=jnp.float32
        )
        grads = grads + jnp.where(valid, term, 0.0)
        previous = lax.dynamic_index_in_dim(stash, slot, 0, keepdims=False)
        stash = lax.dynamic_update_index_in_dim(stash, jnp.where(valid, result, previous), slot, 0)
        arrived = passed_along(result, "segment", 1)
        return (arrived, stash, grads)

    start = (
        jnp.zeros(clips.shape[1:], jnp.bfloat16),
        jnp.zeros(clips.shape, jnp.bfloat16),
        jnp.zeros((27 * chans, chans), jnp.float32),
    )
    arrived, stash, grads = lax.fori_loop(0, micro + segments - 1, tick, start)
    grads = lax.psum(grads, ("rows", "dp")) * factor
    return (stash[None], grads[None])


TAPS = 9


def swapped(value, axis, flip):
    return lax.ppermute(value, axis, [(i, i ^ flip) for i in range(lax.axis_size(axis))])


def group_sum(value):
    lane = lax.broadcasted_iota(jnp.int32, value.shape, 1)
    chans = value.shape[1]
    for step in (1, 2):
        after = pltpu.roll(value, chans - step, 1)
        before = pltpu.roll(value, step, 1)
        value = value + jnp.where(lane & step == 0, after, before)
    return value


def normalized(values, length, gain, shift):
    frames = len(values)
    positions, chans = values[0].shape
    mask = [(length > f).astype(jnp.float32) for f in range(frames)]
    count = length * (positions * (chans // GROUPS))

    def masked_sum(arrays):
        parts = [
            jnp.sum(a.reshape(positions // 8, 8, chans), axis=0) * m for a, m in zip(arrays, mask)
        ]
        return group_sum(jnp.sum(sum(parts), axis=0, keepdims=True))

    mean = masked_sum(values) / count
    centered = [v - mean for v in values]
    var = masked_sum([c * c for c in centered]) / count
    rstd = lax.rsqrt(var + eps)
    normed = [c * rstd * gain + shift for c in centered]
    return [v / (1.0 + jnp.exp(-v)) for v in normed]


def taps_of(hidden, cols):
    positions, lanes = hidden.shape
    rows = positions // cols
    zero = jnp.zeros((1, cols, lanes), jnp.float32)
    padded = jnp.concatenate([zero, hidden.reshape(rows, cols, lanes), zero], axis=0)
    col = lax.broadcasted_iota(jnp.int32, padded.shape, 1)
    left = jnp.where(col == 0, 0.0, pltpu.roll(padded, 1, 1))
    right = jnp.where(col == cols - 1, 0.0, pltpu.roll(padded, cols - 1, 1))
    pieces = [
        value[b : b + rows].reshape(positions, lanes).astype(jnp.bfloat16)
        for b in range(3)
        for value in (left, padded, right)
    ]
    return jnp.concatenate(pieces, axis=1)


def convolved(hidden, weight_ref, cols):
    frames = len(hidden)
    chans = hidden[0].shape[1]
    depth = TAPS * chans
    outs = [None] * frames
    for source in range(frames):
        patch = taps_of(hidden[source], cols)
        uses = [(f, a) for f in range(frames) for a in range(3) if max(f + a - 2, 0) == source]
        needed = sorted({a for _, a in uses})
        weight = jnp.concatenate([weight_ref[a * depth : (a + 1) * depth] for a in needed], axis=1)
        product = jnp.dot(patch, weight, preferred_element_type=jnp.float32)
        for f, a in uses:
            at = needed.index(a) * chans
            term = product[:, at : at + chans]
            outs[f] = term if outs[f] is None else outs[f] + term
    return outs


def real_frames(lengths):
    index = lax.broadcasted_iota(jnp.int32, lengths.shape, 1)
    mine = jnp.where(index == lax.axis_index("rows"), lengths[...].astype(jnp.float32), 0.0)
    return jnp.sum(mine, axis=1, keepdims=True)


def split_three(value):
    high = lax.reduce_precision(value, 8, 7)
    rest = value - high
    middle = lax.reduce_precision(rest, 8, 7)
    return jnp.stack([high, middle, rest - middle]).astype(jnp.bfloat16)


def prepare_kernel(lengths, clips, *refs):
    pieces, (arrived, gain, shift, bias, whole, hidden, params) = refs[:3], refs[3:]
    segment, row = lax.axis_index("segment"), lax.axis_index("rows")
    _, frames, span, chans = pieces[0].shape
    for k, piece in enumerate([clips.at[row], *[p.at[0] for p in pieces]]):
        whole[:, pl.ds(pl.multiple_of((row ^ k) * span, span), span), :] = piece[...]
    extra = arrived[arrived.shape[0] - 16 :].astype(jnp.float32)
    sent = [extra[i : i + 1] + extra[i + 3 : i + 4] + extra[i + 6 : i + 7] for i in range(3)]
    own = (gain, shift, bias)
    used = [jnp.where(segment == 0, o[...], s) for o, s in zip(own, sent)]
    values = [whole[f].astype(jnp.float32) for f in range(frames)]
    out = normalized(values, real_frames(lengths), used[0], used[1])
    for f in range(frames):
        hidden[f] = out[f].astype(jnp.bfloat16)
    params[...] = jnp.broadcast_to(used[2], params.shape)


def first_kernel(
    cols, lengths, whole, hidden, own_weight, arrived, other, params, gain, shift, *refs
):
    (mine, near, far, middle, after, weight) = refs
    slices = [mine, near, far.at[0], far.at[1]]
    segment, part = lax.axis_index("segment"), lax.axis_index("dp")
    frames, positions, chans = whole.shape
    real = real_frames(lengths)
    half = own_weight.shape[0] // 2
    core = part & 1

    @pl.when(segment == 0)
    def _():
        weight[...] = own_weight[...]

    @pl.when(segment != 0)
    def _():
        at = pl.multiple_of(core * half, 16)
        weight[pl.ds(at, half)] = arrived[:half]
        at = pl.multiple_of((1 - core) * half, 16)
        weight[pl.ds(at, half)] = other[:half]

    before = [hidden[f].astype(jnp.float32) for f in range(frames)]
    outs = convolved(before, weight, cols)
    bias = params[0:1]
    values = []
    for f in range(frames):
        out = (whole[f].astype(jnp.float32) + outs[f] + bias) * (real > f).astype(jnp.float32)
        middle[f] = out.astype(jnp.bfloat16)
        values.append(middle[f].astype(jnp.float32))
    out = normalized(values, real, gain[...], shift[...])
    out = [o.astype(jnp.bfloat16).astype(jnp.float32) for o in out]
    for f in range(frames):
        after[f] = out[f].astype(jnp.bfloat16)
    chosen = [jnp.where(segment == 0, b, o) for b, o in zip(before, out)]
    quarter = chans // 4
    group = lax.broadcasted_iota(jnp.int32, (positions, chans), 1) // quarter
    for k in range(4):
        packed = None
        for f in range(frames):
            moved = pltpu.roll(chosen[f], ((f - (part ^ k)) & 3) * quarter, 1)
            packed = moved if packed is None else jnp.where(group == f, moved, packed)
        slices[k][...] = packed.astype(jnp.bfloat16)


def second_kernel(cols, lengths, middle, after, weight, bias, *refs):
    mine, outer, inner, stash = refs
    pieces = [mine, outer.at[0], inner, outer.at[1]]
    segment, row = lax.axis_index("segment"), lax.axis_index("rows")
    frames, positions, chans = middle.shape
    span = positions // 4
    real = real_frames(lengths)

    @pl.when(segment == 0)
    def _():
        stash[...] = middle[...]

    @pl.when(segment != 0)
    def _():
        outs = convolved([after[f].astype(jnp.float32) for f in range(frames)], weight, cols)
        for f in range(frames):
            out = middle[f].astype(jnp.float32) + outs[f] + bias[...]
            stash[f] = (out * (real > f).astype(jnp.float32)).astype(jnp.bfloat16)

    for k, piece in enumerate(pieces):
        piece[...] = stash[:, pl.ds(pl.multiple_of((row ^ k) * span, span), span), :]


def cotangent_kernel(early, late, turned, whole):
    row = lax.axis_index("rows")
    _, frames, span, chans = early.shape
    for k, piece in enumerate([early.at[0], early.at[1], late.at[0], late.at[1]]):
        whole[:, pl.ds(pl.multiple_of((row ^ k) * span, span), span), :] = piece[...]
    for f in range(frames):
        turned[f * chans : (f + 1) * chans] = whole[f].astype(jnp.float32).T.astype(jnp.bfloat16)


def gradient_kernel(cols, *refs):
    slices, cots, (send, keep, grad) = refs[:4], refs[4:8], refs[8:]
    row = lax.axis_index("rows")
    chans = slices[0].shape[1]
    quarter = chans // 4
    patches = jnp.concatenate([taps_of(s[...].astype(jnp.float32), cols) for s in slices], axis=0)
    left = jnp.concatenate([c[...] for c in cots], axis=1)
    product = jnp.dot(left, patches, preferred_element_type=jnp.float32)
    group = lax.broadcasted_iota(jnp.int32, (chans, chans), 1) // quarter
    for tap in range(TAPS):
        total = None
        for f in range(4):
            value = product[f * chans : (f + 1) * chans, tap * chans : (tap + 1) * chans]
            moved = None
            for a in range(3):
                by = (a - max(f + a - 2, 0)) * quarter % chans
                turned = pltpu.roll(value, by, 1) if by else value
                moved = turned if moved is None else jnp.where(group == a, turned, moved)
            total = moved if total is None else total + moved
        total = total.T
        for a in range(3):
            grad[a * TAPS + tap] = total[a * quarter : (a + 1) * quarter]
    low = row & 1
    part = quarter // 2
    there = grad[:, pl.ds(pl.multiple_of((1 - low) * part, part), part), :]
    send[...] = there.reshape(send.shape).astype(jnp.bfloat16)
    keep[...] = grad[:, pl.ds(pl.multiple_of(low * part, part), part), :].reshape(keep.shape)


def finish_kernel(total, lower, across, last, beside, opposite, *refs):
    pieces, (grads, stash, whole, sems) = refs[:4], refs[4:]
    row, part = lax.axis_index("rows"), lax.axis_index("dp")
    taps, chans, _ = whole.shape
    copies = []

    def begin(source, target):
        copies.append(pltpu.make_async_copy(source, target, sems.at[len(copies)]))
        copies[-1].start()

    for k, piece in enumerate(pieces):
        begin(piece, stash.at[row ^ k])
    sources = (total, lower, across, last)
    sources += (beside.at[0], beside.at[1], opposite.at[0], opposite.at[1])
    for first, count in ((0, 10), (10, 10), (20, 7)):
        for n, source in enumerate(sources):
            i, j, k = n >> 2, n >> 1 & 1, n & 1
            at = (part ^ (i + 2 * j)) * 32 + ((row & 1) ^ k) * 16
            value = source[first * 16 : (first + count) * 16].astype(jnp.float32)
            value = value.reshape(count, 16, chans)
            whole[first : first + count, pl.ds(pl.multiple_of(at, 16), 16), :] = value
        begin(whole.at[pl.ds(first, count)], grads.at[pl.ds(first, count)])
    for copy in copies:
        copy.wait()


def whole_clips(clips, lengths, conv_weight, norm_gain, norm_shift, conv_bias, cotangent):
    row = lax.axis_index("rows")
    part = lax.axis_index("dp")
    micro, _, frames, rows_here, cols, chans = clips.shape
    span = rows_here * cols
    positions = span * micro
    total_cells = micro * lax.axis_size("dp") * frames * positions
    factor = 1.0 / math.sqrt(total_cells)
    core = part & 1
    weight = conv_weight[0]
    half = weight.shape[0] // 2
    bf16, f32 = jnp.bfloat16, jnp.float32
    shape = jax.ShapeDtypeStruct
    vmem = pl.BlockSpec(memory_space=pltpu.VMEM)
    params = pltpu.CompilerParams(vmem_limit_bytes=48 * 1024 * 1024)

    def call(kernel, outs, scratch, args):
        return pl.pallas_call(
            kernel,
            out_shape=outs,
            in_specs=[vmem] * len(args),
            out_specs=[vmem] * len(outs),
            scratch_shapes=scratch,
            compiler_params=params,
        )(*args)

    clip_like = shape((frames, positions, chans), bf16)
    piece_like = shape((frames, span, chans), bf16)

    clips_here = clips.reshape(micro, frames, span, chans)
    cot_here = cotangent.reshape(micro, frames, span, chans)
    lengths = jnp.transpose(lengths)

    extras = split_three(jnp.concatenate([norm_gain, norm_shift, conv_bias])).reshape(9, chans)
    extras = jnp.pad(extras, ((0, 7), (0, 0)))
    mine = lax.dynamic_slice_in_dim(weight, core * half, half)
    arrived = lax.ppermute(jnp.concatenate([mine, extras]), "segment", [(0, 1)])

    def both(k):
        sent = [lax.dynamic_index_in_dim(v, row ^ k, 0) for v in (clips_here, cot_here)]
        return swapped(jnp.concatenate(sent), "rows", k)

    pieces = [both(k) for k in (1, 2, 3)]

    length = lax.dynamic_index_in_dim(lengths[0], row, 0, keepdims=False)
    mask = (jnp.arange(frames) < length).astype(bf16)[:, None, None]
    own_cot = lax.dynamic_index_in_dim(cot_here, row, 0, keepdims=False)
    early = jnp.stack([own_cot, pieces[0][1]]) * mask
    early_across = swapped(early, "dp", 2)
    pieces[1:], early_across = lax.optimization_barrier((pieces[1:], early_across))
    late = jnp.stack([pieces[1][1], pieces[2][1]]) * mask
    pieces, late, arrived = lax.optimization_barrier((pieces, late, arrived))
    late_across = swapped(late, "dp", 2)

    def turned(first, second):
        return call(
            cotangent_kernel,
            [shape((frames * chans, positions), bf16)],
            [pltpu.VMEM((frames, positions, chans), bf16)],
            [first, second],
        )[0]

    cots = {0: turned(early, late)}
    cots[1] = swapped(cots[0], "dp", 1)

    other = swapped(arrived, "dp", 1)
    whole, hidden, bias0 = call(
        prepare_kernel,
        [clip_like, clip_like, shape((8, chans), f32)],
        [],
        [lengths, clips_here, *pieces, arrived, norm_gain, norm_shift, conv_bias],
    )

    slice_like = shape((positions, chans), bf16)
    mine, near, far, middle, after = call(
        functools.partial(first_kernel, cols),
        [slice_like, slice_like, shape((2, positions, chans), bf16), clip_like, clip_like],
        [pltpu.VMEM(weight.shape, bf16)],
        [lengths, whole, hidden, weight, arrived, other, bias0, norm_gain, norm_shift],
    )
    far = swapped(far, "dp", 2)

    own_piece, outer, inner = call(
        functools.partial(second_kernel, cols),
        [piece_like, shape((2, *piece_like.shape), bf16), piece_like],
        [pltpu.VMEM((frames, positions, chans), bf16)],
        [lengths, middle, after, weight, conv_bias],
    )
    far, late_across, outer, cots[1] = lax.optimization_barrier(
        (far, late_across, outer, cots[1])
    )
    cots[2] = turned(early_across, late_across)
    cots[3] = swapped(cots[2], "dp", 1)
    near = swapped(jnp.stack([near, far[1]]), "dp", 1)
    outer = swapped(outer, "rows", 1)
    held = [mine, near[0], far[0], near[1]]

    quarter = chans // 4
    rows_sent = 27 * quarter // 2
    send, keep = call(
        functools.partial(gradient_kernel, cols),
        [shape((rows_sent, chans), bf16), shape((rows_sent, chans), f32)],
        [pltpu.VMEM((27, quarter, chans), f32)],
        [*held, *[cots[k] for k in range(4)]],
    )
    send, outer = lax.optimization_barrier((send, outer))
    got = swapped(send, "rows", 1)
    total = (keep + got.astype(f32)).astype(bf16)
    total = (total.astype(f32) + swapped(total, "rows", 2).astype(f32)) * factor
    total = total.astype(bf16)
    total, inner, outer = lax.optimization_barrier((total, inner, outer))
    inner = swapped(jnp.stack([inner, outer[1]]), "rows", 2)
    lower = swapped(total, "rows", 1)
    across = swapped(total, "dp", 2)
    last, inner, across = lax.optimization_barrier((swapped(lower, "dp", 2), inner, across))
    beside = swapped(jnp.stack([total, lower]), "dp", 1)
    opposite = swapped(jnp.stack([across, last]), "dp", 1)
    grads, stash = pl.pallas_call(
        finish_kernel,
        out_shape=[shape((27, chans, chans), f32), shape((micro, frames, span, chans), bf16)],
        in_specs=[vmem] * 10,
        out_specs=[pl.BlockSpec(memory_space=pltpu.HBM)] * 2,
        scratch_shapes=[pltpu.VMEM((27, chans, chans), f32), pltpu.SemaphoreType.DMA((7,))],
        compiler_params=params,
    )(total, lower, across, last, beside, opposite, own_piece, outer[0], inner[0], inner[1])
    return (stash.reshape((1,) + clips.shape), grads.reshape(1, 27 * chans, chans))


def per_device(clips, lengths, conv_weight, norm_gain, norm_shift, conv_bias, cotangent):
    sizes = [lax.axis_size(axis) for axis in ("segment", "rows", "dp")]
    fits = sizes == [2, 4, 4] and clips.shape[0] == 4 and clips.shape[1] == 1
    plan = whole_clips if fits and clips.shape[5] == 128 else relay
    return plan(clips, lengths, conv_weight, norm_gain, norm_shift, conv_bias, cotangent)


def solution(mesh):
    in_specs = (
        P(None, "dp", None, "rows", None, None),
        P(None, "dp"),
        P("segment", None, None),
        P("segment", None),
        P("segment", None),
        P("segment", None),
        P("segment", None, "dp", None, "rows", None, None),
    )
    out_specs = (P("segment", None, "dp", None, "rows", None, None), P("segment", None, None))
    return jax.shard_map(
        per_device, mesh=mesh, in_specs=in_specs, out_specs=out_specs, check_vma=False
    )
```

```python
import functools
import math

import jax
import jax.numpy as jnp
from jax import lax
from jax.experimental import pallas as pl
from jax.experimental.pallas import tpu as pltpu
from jax.sharding import PartitionSpec as P

GROUPS = 32


eps = 1e-06


def extended_2(cells, sides, width):
    for axis, dim in sides:
        count = lax.axis_size(axis)
        ends = count - 1
        head = lax.slice_in_dim(cells, 0, width, axis=dim)
        tail = lax.slice_in_dim(cells, cells.shape[dim] - width, cells.shape[dim], axis=dim)
        cells = jnp.concatenate(
            [
                lax.ppermute(tail, axis, [(i, (i + 1) % count) for i in range(ends)]),
                cells,
                lax.ppermute(head, axis, [((i + 1) % count, i) for i in range(ends)]),
            ],
            axis=dim,
        )
    return cells


def passed_along(block, axis, distance):
    devices = range(lax.axis_size(axis))
    route = [(i - distance, i) for i in devices if i - distance in devices]
    return lax.ppermute(block, axis, route)


def statistics(values, frame_mask, length, height):
    clip_count, frames, rows_here, cols, chans = values.shape
    sub = chans // GROUPS
    grouped = values.reshape(clip_count, frames, rows_here, cols, GROUPS, sub)
    mask_six = frame_mask[:, :, :, :, :, None]
    count = (length * (height * cols * sub)).astype(jnp.float32)[:, None]
    total = lax.psum(jnp.sum(grouped * mask_six, axis=(1, 2, 3, 5)), "rows")
    mean = total / count
    centered = grouped - mean[:, None, None, None, :, None]
    spread = lax.psum(jnp.sum(centered * centered * mask_six, axis=(1, 2, 3, 5)), "rows")
    var = spread / count
    rstd = lax.rsqrt(var + eps)
    mean_chan = jnp.repeat(mean, sub, axis=-1)[:, None, None, None, :]
    rstd_chan = jnp.repeat(rstd, sub, axis=-1)[:, None, None, None, :]
    return (mean_chan, rstd_chan)


def block(current, length, weight, gain, shift, bias, height):
    clip_count, frames, rows_here, cols, chans = current.shape
    values = current.astype(jnp.float32)
    frame_mask = (jnp.arange(frames)[None, :] < length[:, None]).astype(jnp.float32)[
        :, :, None, None, None
    ]
    mean_chan, rstd_chan = statistics(values, frame_mask, length, height)
    hidden = jax.nn.silu((values - mean_chan) * rstd_chan * gain + shift).astype(jnp.bfloat16)
    extended = extended_2(hidden, (("rows", 2),), 1)
    padded = jnp.pad(extended, ((0, 0), (0, 0), (0, 0), (1, 1), (0, 0)))
    padded = jnp.concatenate([padded[:, :1], padded[:, :1], padded], axis=1)
    pieces = []
    for tap_t in range(3):
        for tap_h in range(3):
            for tap_w in range(3):
                pieces.append(
                    padded[
                        :,
                        tap_t : tap_t + frames,
                        tap_h : tap_h + rows_here,
                        tap_w : tap_w + cols,
                        :,
                    ]
                )
    patches = jnp.concatenate(pieces, axis=-1).reshape(-1, 27 * chans)
    conv = jnp.dot(patches, weight, preferred_element_type=jnp.float32).reshape(values.shape)
    result = ((values + conv + bias) * frame_mask).astype(jnp.bfloat16)
    return (result, patches, frame_mask.astype(jnp.bfloat16))


def relay(clips, lengths, conv_weight, norm_gain, norm_shift, conv_bias, cotangent):
    segments = lax.axis_size("segment")
    segment_id = lax.axis_index("segment")
    micro = clips.shape[0]
    frames = clips.shape[2]
    cols = clips.shape[4]
    chans = clips.shape[5]
    height = clips.shape[3] * lax.axis_size("rows")
    weight = conv_weight[0]
    gain = norm_gain[0]
    shift = norm_shift[0]
    bias = conv_bias[0]
    cot_all = cotangent[0]
    total_cells = micro * clips.shape[1] * lax.axis_size("dp") * frames * height * cols
    factor = 1.0 / math.sqrt(total_cells)

    def tick(step, carry):
        arrived, stash, grads = carry
        which = step - segment_id
        valid = (which >= 0) & (which < micro)
        slot = jnp.clip(which, 0, micro - 1)
        fresh = lax.dynamic_index_in_dim(
            clips, jnp.clip(step, 0, micro - 1).astype(jnp.int32), 0, keepdims=False
        )
        current = jnp.where(segment_id == 0, fresh, arrived)
        length = lax.dynamic_index_in_dim(lengths, slot, 0, keepdims=False)
        result, patches, mask_five = block(current, length, weight, gain, shift, bias, height)
        cot_now = lax.dynamic_index_in_dim(cot_all, slot, 0, keepdims=False)
        masked = (cot_now * mask_five).reshape(-1, chans)
        term = lax.dot_general(
            patches, masked, (((0,), (0,)), ((), ())), preferred_element_type=jnp.float32
        )
        grads = grads + jnp.where(valid, term, 0.0)
        previous = lax.dynamic_index_in_dim(stash, slot, 0, keepdims=False)
        stash = lax.dynamic_update_index_in_dim(stash, jnp.where(valid, result, previous), slot, 0)
        arrived = passed_along(result, "segment", 1)
        return (arrived, stash, grads)

    start = (
        jnp.zeros(clips.shape[1:], jnp.bfloat16),
        jnp.zeros(clips.shape, jnp.bfloat16),
        jnp.zeros((27 * chans, chans), jnp.float32),
    )
    arrived, stash, grads = lax.fori_loop(0, micro + segments - 1, tick, start)
    grads = lax.psum(grads, ("rows", "dp")) * factor
    return (stash[None], grads[None])


TAPS = 9


def swapped(value, axis, flip):
    return lax.ppermute(value, axis, [(i, i ^ flip) for i in range(lax.axis_size(axis))])


def group_sum(value):
    lane = lax.broadcasted_iota(jnp.int32, value.shape, 1)
    chans = value.shape[1]
    for step in (1, 2):
        after = pltpu.roll(value, chans - step, 1)
        before = pltpu.roll(value, step, 1)
        value = value + jnp.where(lane & step == 0, after, before)
    return value


def normalized(values, length, gain, shift):
    frames = len(values)
    positions, chans = values[0].shape
    mask = [(length > f).astype(jnp.float32) for f in range(frames)]
    count = length * (positions * (chans // GROUPS))

    def masked_sum(arrays):
        parts = [
            jnp.sum(a.reshape(positions // 8, 8, chans), axis=0) * m for a, m in zip(arrays, mask)
        ]
        return group_sum(jnp.sum(sum(parts), axis=0, keepdims=True))

    mean = masked_sum(values) / count
    centered = [v - mean for v in values]
    var = masked_sum([c * c for c in centered]) / count
    rstd = lax.rsqrt(var + eps)
    normed = [c * rstd * gain + shift for c in centered]
    return [v / (1.0 + jnp.exp(-v)) for v in normed]


def taps_of(hidden, cols):
    positions, lanes = hidden.shape
    rows = positions // cols
    zero = jnp.zeros((1, cols, lanes), jnp.float32)
    padded = jnp.concatenate([zero, hidden.reshape(rows, cols, lanes), zero], axis=0)
    col = lax.broadcasted_iota(jnp.int32, padded.shape, 1)
    left = jnp.where(col == 0, 0.0, pltpu.roll(padded, 1, 1))
    right = jnp.where(col == cols - 1, 0.0, pltpu.roll(padded, cols - 1, 1))
    pieces = [
        value[b : b + rows].reshape(positions, lanes).astype(jnp.bfloat16)
        for b in range(3)
        for value in (left, padded, right)
    ]
    return jnp.concatenate(pieces, axis=1)


def convolved(hidden, weight_of, cols):
    frames = len(hidden)
    chans = hidden[0].shape[1]
    outs = [None] * frames
    for source in range(frames):
        patch = taps_of(hidden[source], cols)
        uses = [(f, a) for f in range(frames) for a in range(3) if max(f + a - 2, 0) == source]
        needed = sorted({a for _, a in uses})
        weight = jnp.concatenate([weight_of(a) for a in needed], axis=1)
        product = jnp.dot(patch, weight, preferred_element_type=jnp.float32)
        for f, a in uses:
            at = needed.index(a) * chans
            term = product[:, at : at + chans]
            outs[f] = term if outs[f] is None else outs[f] + term
    return outs


def real_frames(lengths):
    index = lax.broadcasted_iota(jnp.int32, lengths.shape, 1)
    mine = jnp.where(index == lax.axis_index("rows"), lengths[...].astype(jnp.float32), 0.0)
    return jnp.sum(mine, axis=1, keepdims=True)


def split_three(value):
    high = lax.reduce_precision(value, 8, 7)
    rest = value - high
    middle = lax.reduce_precision(rest, 8, 7)
    return jnp.stack([high, middle, rest - middle]).astype(jnp.bfloat16)


def prepare_kernel(lengths, clips, *refs):
    pieces, (arrived, gain, shift, bias, whole, hidden, params) = refs[:3], refs[3:]
    segment, row = lax.axis_index("segment"), lax.axis_index("rows")
    _, frames, span, chans = pieces[0].shape
    for k, piece in enumerate([clips.at[row], *[p.at[0] for p in pieces]]):
        whole[:, pl.ds(pl.multiple_of((row ^ k) * span, span), span), :] = piece[...]
    extra = arrived[arrived.shape[0] - 16 :].astype(jnp.float32)
    sent = [extra[i : i + 1] + extra[i + 3 : i + 4] + extra[i + 6 : i + 7] for i in range(3)]
    own = (gain, shift, bias)
    used = [jnp.where(segment == 0, o[...], s) for o, s in zip(own, sent)]
    values = [whole[f].astype(jnp.float32) for f in range(frames)]
    out = normalized(values, real_frames(lengths), used[0], used[1])
    for f in range(frames):
        hidden[f] = out[f].astype(jnp.bfloat16)
    params[...] = jnp.broadcast_to(used[2], params.shape)


def first_kernel(
    cols, lengths, whole, hidden, own_weight, arrived, other, params, gain, shift, *refs
):
    (mine, near, far, middle, after, outs) = refs
    slices = [mine, near, far.at[0], far.at[1]]
    segment, part = lax.axis_index("segment"), lax.axis_index("dp")
    frames, positions, chans = whole.shape
    real = real_frames(lengths)
    half = own_weight.shape[0] // 2
    depth = TAPS * chans
    core = part & 1
    before = [hidden[f].astype(jnp.float32) for f in range(frames)]

    def run(weight_of):
        for f, out in enumerate(convolved(before, weight_of, cols)):
            outs[f] = out

    def joined(first, second):
        def weight_of(a):
            parts = [first[min(a * depth, half) : min((a + 1) * depth, half)]]
            parts.append(second[max(a * depth - half, 0) : max((a + 1) * depth - half, 0)])
            parts = [p for p in parts if p.shape[0]]
            return parts[0] if len(parts) == 1 else jnp.concatenate(parts, axis=0)

        return weight_of

    @pl.when(segment == 0)
    def _():
        run(lambda a: own_weight[a * depth : (a + 1) * depth])

    @pl.when((segment != 0) & (core == 0))
    def _():
        run(joined(arrived, other))

    @pl.when((segment != 0) & (core != 0))
    def _():
        run(joined(other, arrived))

    bias = params[0:1]
    values = []
    for f in range(frames):
        out = (whole[f].astype(jnp.float32) + outs[f] + bias) * (real > f).astype(jnp.float32)
        middle[f] = out.astype(jnp.bfloat16)
        values.append(middle[f].astype(jnp.float32))
    out = normalized(values, real, gain[...], shift[...])
    out = [o.astype(jnp.bfloat16).astype(jnp.float32) for o in out]
    for f in range(frames):
        after[f] = out[f].astype(jnp.bfloat16)
    chosen = [jnp.where(segment == 0, b, o) for b, o in zip(before, out)]
    quarter = chans // 4
    group = lax.broadcasted_iota(jnp.int32, (positions, chans), 1) // quarter
    for k in range(4):
        packed = None
        for f in range(frames):
            moved = pltpu.roll(chosen[f], ((f - (part ^ k)) & 3) * quarter, 1)
            packed = moved if packed is None else jnp.where(group == f, moved, packed)
        slices[k][...] = packed.astype(jnp.bfloat16)


def second_kernel(cols, lengths, middle, after, weight, bias, *refs):
    mine, outer, inner, stash = refs
    pieces = [mine, outer.at[0], inner, outer.at[1]]
    segment, row = lax.axis_index("segment"), lax.axis_index("rows")
    frames, positions, chans = middle.shape
    span = positions // 4
    real = real_frames(lengths)

    @pl.when(segment == 0)
    def _():
        stash[...] = middle[...]

    @pl.when(segment != 0)
    def _():
        depth = TAPS * chans
        values = [after[f].astype(jnp.float32) for f in range(frames)]
        outs = convolved(values, lambda a: weight[a * depth : (a + 1) * depth], cols)
        for f in range(frames):
            out = middle[f].astype(jnp.float32) + outs[f] + bias[...]
            stash[f] = (out * (real > f).astype(jnp.float32)).astype(jnp.bfloat16)

    for k, piece in enumerate(pieces):
        piece[...] = stash[:, pl.ds(pl.multiple_of((row ^ k) * span, span), span), :]


def cotangent_kernel(early, late, turned, whole):
    row = lax.axis_index("rows")
    _, frames, span, chans = early.shape
    for k, piece in enumerate([early.at[0], early.at[1], late.at[0], late.at[1]]):
        whole[:, pl.ds(pl.multiple_of((row ^ k) * span, span), span), :] = piece[...]
    for f in range(frames):
        turned[f * chans : (f + 1) * chans] = whole[f].astype(jnp.float32).T.astype(jnp.bfloat16)


def gradient_kernel(cols, *refs):
    slices, cots, (send, keep, grad) = refs[:4], refs[4:8], refs[8:]
    row = lax.axis_index("rows")
    chans = slices[0].shape[1]
    quarter = chans // 4
    patches = jnp.concatenate([taps_of(s[...].astype(jnp.float32), cols) for s in slices], axis=0)
    left = jnp.concatenate([c[...] for c in cots], axis=1)
    product = jnp.dot(left, patches, preferred_element_type=jnp.float32)
    group = lax.broadcasted_iota(jnp.int32, (chans, chans), 1) // quarter
    for tap in range(TAPS):
        total = None
        for f in range(4):
            value = product[f * chans : (f + 1) * chans, tap * chans : (tap + 1) * chans]
            moved = None
            for a in range(3):
                by = (a - max(f + a - 2, 0)) * quarter % chans
                turned = pltpu.roll(value, by, 1) if by else value
                moved = turned if moved is None else jnp.where(group == a, turned, moved)
            total = moved if total is None else total + moved
        total = total.T
        for a in range(3):
            grad[a * TAPS + tap] = total[a * quarter : (a + 1) * quarter]
    low = row & 1
    part = quarter // 2
    there = grad[:, pl.ds(pl.multiple_of((1 - low) * part, part), part), :]
    send[...] = there.reshape(send.shape).astype(jnp.bfloat16)
    keep[...] = grad[:, pl.ds(pl.multiple_of(low * part, part), part), :].reshape(keep.shape)


def finish_kernel(total, lower, across, last, beside, opposite, *refs):
    pieces, (grads, stash) = refs[:4], refs[4:]
    row, part = lax.axis_index("rows"), lax.axis_index("dp")
    taps = grads.shape[0]
    sources = (total, lower, across, last)
    sources += (beside.at[0], beside.at[1], opposite.at[0], opposite.at[1])
    for n, source in enumerate(sources):
        i, j, k = n >> 2, n >> 1 & 1, n & 1
        at = (part ^ (i + 2 * j)) * 32 + ((row & 1) ^ k) * 16
        value = source[...].astype(jnp.float32).reshape(taps, 16, grads.shape[2])
        grads[:, pl.ds(pl.multiple_of(at, 16), 16), :] = value
    for k, piece in enumerate(pieces):
        stash[pl.ds(row ^ k, 1)] = piece[...][None]


def whole_clips(clips, lengths, conv_weight, norm_gain, norm_shift, conv_bias, cotangent):
    row = lax.axis_index("rows")
    part = lax.axis_index("dp")
    micro, _, frames, rows_here, cols, chans = clips.shape
    span = rows_here * cols
    positions = span * micro
    total_cells = micro * lax.axis_size("dp") * frames * positions
    factor = 1.0 / math.sqrt(total_cells)
    core = part & 1
    weight = conv_weight[0]
    half = weight.shape[0] // 2
    bf16, f32 = jnp.bfloat16, jnp.float32
    shape = jax.ShapeDtypeStruct
    vmem = pl.BlockSpec(memory_space=pltpu.VMEM)
    params = pltpu.CompilerParams(vmem_limit_bytes=48 * 1024 * 1024)

    def call(kernel, outs, scratch, args):
        return pl.pallas_call(
            kernel,
            out_shape=outs,
            in_specs=[vmem] * len(args),
            out_specs=[vmem] * len(outs),
            scratch_shapes=scratch,
            compiler_params=params,
        )(*args)

    clip_like = shape((frames, positions, chans), bf16)
    piece_like = shape((frames, span, chans), bf16)

    clips_here = clips.reshape(micro, frames, span, chans)
    cot_here = cotangent.reshape(micro, frames, span, chans)
    lengths = jnp.transpose(lengths)

    extras = split_three(jnp.concatenate([norm_gain, norm_shift, conv_bias])).reshape(9, chans)
    extras = jnp.pad(extras, ((0, 7), (0, 0)))
    mine = lax.dynamic_slice_in_dim(weight, core * half, half)
    arrived = lax.ppermute(jnp.concatenate([mine, extras]), "segment", [(0, 1)])

    def both(k):
        sent = [lax.dynamic_index_in_dim(v, row ^ k, 0) for v in (clips_here, cot_here)]
        return swapped(jnp.concatenate(sent), "rows", k)

    pieces = [both(k) for k in (1, 2, 3)]

    length = lax.dynamic_index_in_dim(lengths[0], row, 0, keepdims=False)
    mask = (jnp.arange(frames) < length).astype(bf16)[:, None, None]
    own_cot = lax.dynamic_index_in_dim(cot_here, row, 0, keepdims=False)
    early = jnp.stack([own_cot, pieces[0][1]]) * mask
    early_across = swapped(early, "dp", 2)
    pieces[1:], early_across = lax.optimization_barrier((pieces[1:], early_across))
    late = jnp.stack([pieces[1][1], pieces[2][1]]) * mask
    pieces, late, arrived = lax.optimization_barrier((pieces, late, arrived))
    late_across = swapped(late, "dp", 2)

    def turned(first, second):
        return call(
            cotangent_kernel,
            [shape((frames * chans, positions), bf16)],
            [pltpu.VMEM((frames, positions, chans), bf16)],
            [first, second],
        )[0]

    cots = {0: turned(early, late)}
    cots[1] = swapped(cots[0], "dp", 1)

    other = swapped(arrived, "dp", 1)
    whole, hidden, bias0 = call(
        prepare_kernel,
        [clip_like, clip_like, shape((8, chans), f32)],
        [],
        [lengths, clips_here, *pieces, arrived, norm_gain, norm_shift, conv_bias],
    )

    slice_like = shape((positions, chans), bf16)
    mine, near, far, middle, after = call(
        functools.partial(first_kernel, cols),
        [slice_like, slice_like, shape((2, positions, chans), bf16), clip_like, clip_like],
        [pltpu.VMEM((frames, positions, chans), f32)],
        [lengths, whole, hidden, weight, arrived, other, bias0, norm_gain, norm_shift],
    )
    far = swapped(far, "dp", 2)

    own_piece, outer, inner = call(
        functools.partial(second_kernel, cols),
        [piece_like, shape((2, *piece_like.shape), bf16), piece_like],
        [pltpu.VMEM((frames, positions, chans), bf16)],
        [lengths, middle, after, weight, conv_bias],
    )
    far, late_across, outer, cots[1] = lax.optimization_barrier(
        (far, late_across, outer, cots[1])
    )
    cots[2] = turned(early_across, late_across)
    cots[3] = swapped(cots[2], "dp", 1)
    near = swapped(jnp.stack([near, far[1]]), "dp", 1)
    outer = swapped(outer, "rows", 1)
    held = [mine, near[0], far[0], near[1]]

    quarter = chans // 4
    rows_sent = 27 * quarter // 2
    send, keep = call(
        functools.partial(gradient_kernel, cols),
        [shape((rows_sent, chans), bf16), shape((rows_sent, chans), f32)],
        [pltpu.VMEM((27, quarter, chans), f32)],
        [*held, *[cots[k] for k in range(4)]],
    )
    send, outer = lax.optimization_barrier((send, outer))
    got = swapped(send, "rows", 1)
    total = (keep + got.astype(f32)).astype(bf16)
    total = (total.astype(f32) + swapped(total, "rows", 2).astype(f32)) * factor
    total = total.astype(bf16)
    total, inner, outer = lax.optimization_barrier((total, inner, outer))
    inner = swapped(jnp.stack([inner, outer[1]]), "rows", 2)
    lower = swapped(total, "rows", 1)
    across = swapped(total, "dp", 2)
    last, inner, across = lax.optimization_barrier((swapped(lower, "dp", 2), inner, across))
    beside = swapped(jnp.stack([total, lower]), "dp", 1)
    opposite = swapped(jnp.stack([across, last]), "dp", 1)
    grads, stash = call(
        finish_kernel,
        [shape((27, chans, chans), f32), shape((micro, frames, span, chans), bf16)],
        [],
        [
            *[total, lower, across, last, beside, opposite],
            *[own_piece, outer[0], inner[0], inner[1]],
        ],
    )
    return (stash.reshape((1,) + clips.shape), grads.reshape(1, 27 * chans, chans))


def per_device(clips, lengths, conv_weight, norm_gain, norm_shift, conv_bias, cotangent):
    sizes = [lax.axis_size(axis) for axis in ("segment", "rows", "dp")]
    fits = sizes == [2, 4, 4] and clips.shape[0] == 4 and clips.shape[1] == 1
    plan = whole_clips if fits and clips.shape[5] == 128 else relay
    return plan(clips, lengths, conv_weight, norm_gain, norm_shift, conv_bias, cotangent)


def solution(mesh):
    in_specs = (
        P(None, "dp", None, "rows", None, None),
        P(None, "dp"),
        P("segment", None, None),
        P("segment", None),
        P("segment", None),
        P("segment", None),
        P("segment", None, "dp", None, "rows", None, None),
    )
    out_specs = (P("segment", None, "dp", None, "rows", None, None), P("segment", None, None))
    return jax.shard_map(
        per_device, mesh=mesh, in_specs=in_specs, out_specs=out_specs, check_vma=False
    )
```
